256 devices in a mesh: dp: 64 (over z, x, y_lo), section: 4 (over y_hi, core).
Axes of the slice: x: 4, y: 4 (y_hi: 2, y_lo: 2; y = y_hi * 2 + y_lo), z: 8, core: 2. Of those that a mesh axis runs over, the one named last changes fastest.
Arguments:
- acts: bfloat16 [4, 16384, 1152], P('section', 'dp'), may hold values from -6 to 6
- grad_in: bfloat16 [4, 16384, 1152], P('section', 'dp'), may hold values from -16 to 16
- gain: float32 [4, 1152], P('section'), may hold values from 0.1 to 1.9
- w_in: bfloat16 [4, 1152, 2176], P('section', 'dp'), may hold values from -0.1875 to 0.1875
- w_out: bfloat16 [4, 1152, 2176], P('section', 'dp'), may hold values from -0.125 to 0.125
Outputs:
- handed: bfloat16 [4, 16384, 1152], P('section', 'dp')
- grad_w_in: float32 [4, 1152, 2176], P('section', 'dp')
- grad_w_out: float32 [4, 1152, 2176], P('section', 'dp')
- grad_gain: float32 [4, 1152], P('section')
The draws below stay inside these ranges and needn't reach their ends.
All inputs are finite; a program needn't handle non-finite values.
Results may differ from the reference program's by a relative error of at most 0.0055.
Values may be sent and summed in bfloat16 or wider, within the bound.
No kernel may reach another device: no remote copies, remote signals or barrier semaphores. Data moves between devices by JAX's collectives and lax.ppermute only.
A program may use at most 128 MiB of HBM per device.

```python
import jax
import jax.numpy as jnp
from jax import lax

D = 1152
HID = 2176
TOKENS = 16384
SECTIONS = 4


def raised(entries, stream_key, source, target, parts, factor):
    def block_of(position):
        return (jnp.arange(entries.shape[position]) // (entries.shape[position] // parts)).reshape((-1,) + (1,) * (entries.ndim - 1 - position))

    near = jax.random.permutation(stream_key, parts)[block_of(target)]
    far = (block_of(target) + parts // 2) % parts
    return jnp.where((block_of(source) == near) | (block_of(source) == far), factor * entries, entries)


def block_scale(rng, shape, cuts, least, high):
    level = 1.0
    for position, parts in cuts:
        heights = jax.random.uniform(jax.random.fold_in(jax.random.fold_in(rng, 6), position), (parts,), jnp.float32, least / len(cuts), high / len(cuts))
        level = level * jnp.repeat(jnp.exp(heights), shape[position] // parts).reshape((-1,) + (1,) * (len(shape) - 1 - position))
    return level


def gaussian(rng, shape, width, reach, pieces=(), kind=jnp.bfloat16):
    level = block_scale(rng, shape, pieces, -0.22, 0.18) if pieces else 1.0
    array = jax.random.normal(rng, shape, jnp.float32) * width * level
    return jnp.minimum(jnp.maximum(array, -reach), reach).astype(kind)


def noise_with(key, shape, scale, reach, shards, heavy, kind=jnp.bfloat16):
    values = scale * jax.random.normal(key, shape, jnp.float32)
    if shards:
        values = values * block_scale(key, shape, shards, -0.22, 0.18)
    return jnp.clip(raised(values, jax.random.fold_in(key, 3), *heavy), -reach, reach).astype(kind)


def setup_inputs(seed: int = 0) -> dict:
    seeds = jax.random.split(jax.random.key(seed), 6)
    return {
        "acts": gaussian(seeds[0], (SECTIONS, TOKENS, D), 1.0, 6.0, ((0, 4), (1, 64))),
        "grad_in": noise_with(seeds[1], (SECTIONS, TOKENS, D), 1.0, 16.0, ((0, 4), (1, 64)), (1, 2, 64, 4.0)),
        "gain": jnp.clip(1.0 + 0.18 * jax.random.normal(seeds[2], (SECTIONS, D), jnp.float32), 0.1, 1.9),
        "w_in": gaussian(seeds[3], (SECTIONS, D, HID), D ** -0.5, 0.1875, ((0, 4), (1, 64))),
        "w_out": gaussian(seeds[4], (SECTIONS, D, HID), HID ** -0.5, 0.125, ((0, 4), (1, 64))),
    }


coef = 0.7978845608

def gelu_value(pre):
    inner = jnp.tanh(coef * (pre + 0.044715 * pre * pre * pre))
    return 0.5 * pre * (1.0 + inner)

def gelu_slope(pre):
    inner = jnp.tanh(coef * (pre + 0.044715 * pre * pre * pre))
    return 0.5 * (1.0 + inner) + 0.5 * pre * (1.0 - inner * inner) * coef * (1.0 + 0.134145 * pre * pre)

def one_section(acts_s, grad_s, gain_s, w_in_s, w_out_s, scale):
    source = acts_s.astype(jnp.float32)
    mean_row = lax.optimization_barrier(jnp.mean(source, axis=1, keepdims=True))
    centred = source - mean_row
    inv = 1.0 / jnp.sqrt(lax.optimization_barrier(jnp.mean(centred * centred, axis=1, keepdims=True)) + 1e-06)
    normed = centred * inv
    scaled = (normed * gain_s[None, :]).astype(jnp.bfloat16)
    pre = jnp.dot(scaled, w_in_s, preferred_element_type=jnp.float32)
    hidden = gelu_value(pre).astype(jnp.bfloat16)
    dhidden = jnp.dot(grad_s, w_out_s, preferred_element_type=jnp.float32)
    dpre = (dhidden * gelu_slope(pre)).astype(jnp.bfloat16)
    dims = (((0,), (0,)), ((), ()))
    grad_out = lax.dot_general(grad_s, hidden, dims, preferred_element_type=jnp.float32) * scale
    grad_inw = lax.dot_general(scaled, dpre, dims, preferred_element_type=jnp.float32) * scale
    dscaled = lax.dot_general(dpre, w_in_s, (((1,), (1,)), ((), ())), preferred_element_type=jnp.float32)
    grad_g = lax.optimization_barrier(jnp.sum(dscaled * normed, axis=0)) * scale
    dnormed = dscaled * gain_s[None, :]
    grad_x = grad_s.astype(jnp.float32) + inv * (dnormed - lax.optimization_barrier(jnp.mean(dnormed, axis=1, keepdims=True)) - normed * lax.optimization_barrier(jnp.mean(dnormed * normed, axis=1, keepdims=True)))
    return (grad_x.astype(jnp.bfloat16), grad_inw, grad_out, grad_g)

def reference(acts, grad_in, gain, w_in, w_out):
    scale = 1.0 / jnp.sqrt(jnp.float32(TOKENS))
    grad_xs = []
    grad_ins = []
    grad_outs = []
    grad_gains = []
    for section_no in range(SECTIONS):
        grad_x, grad_inw, grad_out, grad_g = one_section(acts[section_no], grad_in[section_no], gain[section_no], w_in[section_no], w_out[section_no], scale)
        grad_xs.append(grad_x)
        grad_ins.append(grad_inw)
        grad_outs.append(grad_out)
        grad_gains.append(grad_g)
    handed = jnp.stack(grad_xs[1:] + grad_xs[:1])
    return (handed, jnp.stack(grad_ins), jnp.stack(grad_outs), jnp.stack(grad_gains))
```

```python
import jax
import jax.numpy as jnp
from jax import lax
from jax.sharding import Mesh, PartitionSpec as P

coef = 0.7978845608
f32, bf16 = jnp.float32, jnp.bfloat16


def shift(block, axis, distance):
    size = lax.axis_size(axis)
    return lax.ppermute(block, axis, [(i, (i + distance) % size) for i in range(size)])


SWAP = [(2 * y + c, 2 * c + y) for y in range(2) for c in range(2)]
OUT_CROSS = [(2 * y + c, 2 * c + 1 - y) for y in range(2) for c in range(2)]
BACK_CROSS = [(b, a) for a, b in OUT_CROSS]


def pick(flag, a, b):
    return jnp.where(flag == 0, a, b), jnp.where(flag == 0, b, a)


def direct_gather(block, axis):
    size = lax.axis_size(axis)
    me = lax.axis_index(axis)
    out = jnp.zeros((size,) + block.shape, block.dtype)
    out = lax.dynamic_update_index_in_dim(out, block, me, 0)
    for k in range(1, size):
        got = shift(block, axis, k)
        out = lax.dynamic_update_index_in_dim(out, got, (me - k) % size, 0)
    return out


def direct_scatter(blocks, axis):
    size = lax.axis_size(axis)
    me = lax.axis_index(axis)
    total = lax.dynamic_index_in_dim(blocks, me, 0, keepdims=False).astype(f32)
    for k in range(1, size):
        part = lax.dynamic_index_in_dim(blocks, (me + k) % size, 0, keepdims=False)
        total = total + shift(part, axis, k).astype(f32)
    return total


def dot(a, b, ca, cb):
    return lax.dot_general(a, b, (((ca,), (cb,)), ((), ())), preferred_element_type=f32)


def local(nz, nx, acts, grad_in, gain, w_in, w_out):
    y, c = lax.axis_index("y"), lax.axis_index("c")
    rows, hid = w_in.shape[1:]
    half = hid // 2
    d = acts.shape[2]
    tokens = acts.shape[1]
    scale = 1.0 / jnp.sqrt(jnp.float32(tokens * nz * nx * 2))

    both = jnp.concatenate([w_in, w_out], axis=0)
    low, high = both[:, :, :half], both[:, :, half:]
    same, cross = pick(y, low, high)
    same = lax.ppermute(same, ("y", "c"), SWAP)
    cross = lax.ppermute(cross, ("y", "c"), OUT_CROSS)
    top, bottom = pick(c, same, cross)
    shard = jnp.concatenate([top, bottom], axis=1)
    first = direct_gather(shard[0], "x").reshape(nx * 2 * rows, half)
    first = lax.all_gather(first, "z", axis=0, tiled=True)
    second = lax.all_gather(shard[1], "z", axis=0, tiled=False)
    second = direct_gather(second, "x")
    second = second.transpose(1, 0, 2, 3).reshape(d, half)

    acts_s = lax.ppermute(acts[0], ("y", "c"), SWAP)
    grad_own = lax.ppermute(grad_in[0], ("y", "c"), SWAP)
    gain_s = lax.ppermute(gain[0], ("y", "c"), SWAP)
    source = acts_s.astype(f32)
    centred = source - jnp.mean(source, axis=1, keepdims=True)
    inv = 1.0 / jnp.sqrt(jnp.mean(centred * centred, axis=1, keepdims=True) + 1e-06)
    normed = centred * inv
    scaled_own = (normed * gain_s[None, :]).astype(bf16)
    scaled = jnp.concatenate([scaled_own, shift(scaled_own, "c", 1)], axis=0)
    grads = jnp.concatenate([grad_own, shift(grad_own, "c", 1)], axis=0)

    pre = dot(scaled, first, 1, 0)
    th = jnp.tanh(coef * (pre + 0.044715 * pre * pre * pre))
    hidden = (0.5 * pre * (1.0 + th)).astype(bf16)
    slope = 0.5 * (1.0 + th) + 0.5 * pre * (1.0 - th * th) * coef * (
        1.0 + 0.134145 * pre * pre
    )
    out_term = dot(grads, hidden, 0, 0).astype(bf16)
    sum_out = lax.psum_scatter(out_term, "z", scatter_dimension=0, tiled=True)
    sum_out = direct_scatter(sum_out.reshape(nx, 2 * rows, half), "x")

    dpre = (dot(grads, second, 1, 0) * slope).astype(bf16)
    in_term = dot(scaled, dpre, 0, 0).astype(bf16)
    in_term = in_term.reshape(nz, nx, 2 * rows, half).transpose(1, 0, 2, 3)
    sum_in = direct_scatter(in_term, "x").astype(bf16)
    sum_in = lax.all_to_all(sum_in, "z", 0, 0)
    sum_in = jnp.sum(sum_in.astype(f32), axis=0)

    sums = jnp.stack([sum_in, sum_out]) * scale
    same, cross = pick(c, sums[:, :rows], sums[:, rows:])
    same = lax.ppermute(same, ("y", "c"), SWAP)
    cross = lax.ppermute(cross, ("y", "c"), BACK_CROSS)
    low, high = pick(y, same, cross)
    grad_w = jnp.concatenate([low, high], axis=2)

    partial = dot(dpre, first, 1, 1)
    dscaled = partial[:tokens] + shift(partial[tokens:], "c", 1)
    grad_g = lax.psum(jnp.sum(dscaled * normed, axis=0), ("z", "x", "c")) * scale
    grad_g = lax.ppermute(grad_g, ("y", "c"), SWAP)
    dnormed = dscaled * gain_s[None, :]
    grad_x = grad_own.astype(f32) + inv * (
        dnormed
        - jnp.mean(dnormed, axis=1, keepdims=True)
        - normed * jnp.mean(dnormed * normed, axis=1, keepdims=True)
    )
    route = []
    for yy in range(2):
        for hh in range(2):
            for cc in range(2):
                to = (2 * hh + yy - 1) % 4
                route.append((4 * yy + 2 * hh + cc, 4 * cc + 2 * (to // 2) + to % 2))
    handed = lax.ppermute(grad_x.astype(bf16), ("y", "h", "c"), route)
    return handed[None], grad_w[0][None], grad_w[1][None], grad_g[None]


def solution(mesh):
    nz, nx = 8, mesh.shape["dp"] // 16
    fine = Mesh(mesh.devices.reshape(nz, nx, 2, 2, 2), ("z", "x", "y", "h", "c"))
    wide = P(("h", "c"), ("z", "x", "y"), None)
    slim = P(("h", "c"), None)

    def run(*args):
        return local(nz, nx, *args)

    return jax.shard_map(
        run,
        mesh=fine,
        in_specs=(wide, wide, slim, wide, wide),
        out_specs=(wide, wide, wide, slim),
        check_vma=False,
    )
```

```python
import jax
import jax.numpy as jnp
from jax import lax
from jax.experimental import pallas as pl
from jax.experimental.pallas import tpu as pltpu
from jax.sharding import Mesh, PartitionSpec as P

coef = 0.7978845608
f32, bf16 = jnp.float32, jnp.bfloat16

SLOTS = (0, 1, 3, 2)
PAD = 40
VMEM = pltpu.CompilerParams(vmem_limit_bytes=56 * 1024 * 1024)


def shift(block, axis, distance):
    size = lax.axis_size(axis)
    return lax.ppermute(block, axis, [(i, (i + distance) % size) for i in range(size)])


def pick(flag, a, b):
    return jnp.where(flag == 0, a, b), jnp.where(flag == 0, b, a)


def ring_gather(block, axis):
    size, r = lax.axis_size(axis), block.shape[0]
    me = lax.axis_index(axis)
    out = jnp.zeros((size * r, block.shape[1]), block.dtype)
    out = lax.dynamic_update_slice(out, block, (me * r, 0))
    right = left = block
    for k in range(1, size // 2 + 1):
        right = shift(right, axis, 1)
        out = lax.dynamic_update_slice(out, right, ((me - k) % size * r, 0))
        if k < size - k:
            left = shift(left, axis, -1)
            out = lax.dynamic_update_slice(out, left, ((me + k) % size * r, 0))
    return out


def direct_gather(block, axis):
    size = lax.axis_size(axis)
    me = lax.axis_index(axis)
    out = jnp.zeros((size,) + block.shape, block.dtype)
    out = lax.dynamic_update_index_in_dim(out, block, me, 0)
    for k in range(1, size):
        got = shift(block, axis, k)
        out = lax.dynamic_update_index_in_dim(out, got, (me - k) % size, 0)
    return out


def dot(a, b, ca=1, cb=0):
    return lax.dot_general(a, b, (((ca,), (cb,)), ((), ())), preferred_element_type=f32)


def tiles(width):
    starts = list(range(0, width - 255, 256))
    ends = starts[1:] + [width]
    return list(zip(starts, ends))


def up_kernel(scaled, first, grads_t, slope, out_term):
    for a, b in tiles(first.shape[1]):
        pre = dot(scaled[...], first[:, a:b])
        th = jnp.tanh(coef * (pre + 0.044715 * pre * pre * pre))
        slope[:, a:b] = 0.5 * (1.0 + th) + 0.5 * pre * (1.0 - th * th) * coef * (
            1.0 + 0.134145 * pre * pre
        )
        hidden = (0.5 * pre * (1.0 + th)).astype(bf16)
        out_term[:, a:b] = dot(grads_t[...], hidden).astype(bf16)


def down_kernel(grads, s0, s1, s2, s3, slope, scaled_t, dpre, o0, o1, o2, o3, second, sem):
    rows = s0.shape[0]
    copies = [
        pltpu.make_async_copy(s, second.at[pl.ds(rows * j, rows)], sem.at[j])
        for j, s in enumerate((s0, s1, s2, s3))
    ]
    for copy in copies:
        copy.start()
    for copy in copies:
        copy.wait()
    for a, b in tiles(second.shape[1]):
        part = (dot(grads[...], second[:, a:b]) * slope[:, a:b]).astype(bf16)
        dpre[:, a:b] = part
        for j, out in enumerate((o0, o1, o2, o3)):
            out[:, a:b] = dot(scaled_t[rows * j : rows * (j + 1)], part).astype(bf16)


def up(scaled, first, grads_t):
    t, d = scaled.shape
    half = first.shape[1]
    return pl.pallas_call(
        up_kernel,
        out_shape=(
            jax.ShapeDtypeStruct((t, half), f32),
            jax.ShapeDtypeStruct((d, half), bf16),
        ),
        compiler_params=VMEM,
        cost_estimate=pl.CostEstimate(
            flops=4 * t * d * half, bytes_accessed=4 * d * half, transcendentals=t * half
        ),
    )(scaled, first, grads_t)


def down(grads, slots, slope, scaled_t):
    t, wide = grads.shape
    rows, half = slots[0].shape
    whole = pl.BlockSpec(memory_space=pltpu.VMEM)
    away = pl.BlockSpec(memory_space=pl.ANY)
    return pl.pallas_call(
        down_kernel,
        out_shape=(jax.ShapeDtypeStruct((t, half), bf16),)
        + (jax.ShapeDtypeStruct((rows, half), bf16),) * 4,
        in_specs=[whole] + [away] * 4 + [whole] * 2,
        out_specs=(whole,) * 5,
        scratch_shapes=[pltpu.VMEM((wide, half), bf16), pltpu.SemaphoreType.DMA((4,))],
        compiler_params=VMEM,
        cost_estimate=pl.CostEstimate(
            flops=4 * t * wide * half, bytes_accessed=4 * wide * half, transcendentals=0
        ),
    )(grads, *slots, slope, scaled_t)


def turned(matrix, x, nz, nx):
    t, d = matrix.shape
    rows = d // (nz * nx)
    blocks = matrix.T.reshape(nz, nx, rows, t)
    blocks = jnp.stack(
        [lax.dynamic_index_in_dim(blocks, (x + o) % nx, 1, keepdims=False) for o in SLOTS]
    )
    blocks = jnp.pad(blocks, ((0, 0), (0, 0), (0, PAD - rows), (0, 0)))
    return blocks.reshape(nx * nz * PAD, t)


def local(nz, nx, acts, grad_in, gain, w_in, w_out):
    x, y = lax.axis_index("x"), lax.axis_index("y")
    rows, hid = w_in.shape[1:]
    half = hid // 2
    tokens, d = acts.shape[1:]
    scale = 1.0 / jnp.sqrt(jnp.float32(tokens * nz * nx * 2))

    both = jnp.concatenate([w_in, w_out], axis=0)
    mine, theirs = pick(y, both[:, :, :half], both[:, :, half:])
    top, bottom = pick(y, mine, shift(theirs, "y", 1))
    shard = jnp.concatenate([top, bottom], axis=1)
    first = direct_gather(shard[0], "x").reshape(nx * 2 * rows, half)
    first = lax.all_gather(first, "z", axis=0, tiled=True)
    second = ring_gather(jnp.pad(shard[1], ((0, PAD - 2 * rows), (0, 0))), "z")
    slots = [second] + [shift(second, "x", -o) for o in SLOTS[1:]]

    source = acts[0].astype(f32)
    centred = source - jnp.mean(source, axis=1, keepdims=True)
    inv = 1.0 / jnp.sqrt(jnp.mean(centred * centred, axis=1, keepdims=True) + 1e-06)
    normed = centred * inv
    scaled = (normed * gain[0][None, :]).astype(bf16)
    scaled = jnp.concatenate([scaled, shift(scaled, "y", 1)], axis=0)
    grads = jnp.concatenate([grad_in[0], shift(grad_in[0], "y", 1)], axis=0)
    scaled_t = turned(scaled, x, nz, nx)
    grads_w = turned(grads, x, nz, nx).T

    slope, out_term = up(scaled, first, grads.T)
    sum_out = lax.psum_scatter(out_term, "z", scatter_dimension=0, tiled=True)
    sum_out = sum_out.reshape(nx, 2 * rows, half)
    total_out = lax.dynamic_index_in_dim(sum_out, x, 0, keepdims=False).astype(f32)
    for o in SLOTS[1:]:
        part = lax.dynamic_index_in_dim(sum_out, (x + o) % nx, 0, keepdims=False)
        total_out += shift(part, "x", o).astype(f32)

    def returned(total, extra):
        total = total * scale
        keep, send = pick(y, total[:rows], total[rows:])
        if extra is not None:
            send = jnp.concatenate([send, extra], axis=0)
        got = shift(send, "y", 1)
        low, high = pick(y, keep, got[:rows])
        return jnp.concatenate([low, high], axis=1), got[rows:]

    grad_out, _ = returned(total_out, None)

    dpre, *terms = down(grads_w, slots, slope, scaled_t)
    total_in = terms[0].astype(f32)
    for o, term in zip(SLOTS[1:], terms[1:]):
        total_in += shift(term, "x", o).astype(f32)

    partial = dot(dpre, first, 1, 1)
    dscaled = partial[:tokens] + shift(partial[tokens:].astype(bf16), "y", 1).astype(f32)
    grad_g = jnp.sum(dscaled * normed, axis=0, keepdims=True) * scale
    dnormed = dscaled * gain[0][None, :]
    grad_x = grad_in[0].astype(f32) + inv * (
        dnormed
        - jnp.mean(dnormed, axis=1, keepdims=True)
        - normed * jnp.mean(dnormed * normed, axis=1, keepdims=True)
    )
    route = [(2 * h + c, (2 * h + c - 1) % 4) for h in range(2) for c in range(2)]
    handed = lax.ppermute(grad_x.astype(bf16), ("h", "c"), route)

    grad_g = sum([shift(grad_g, "x", o) for o in SLOTS[1:]], grad_g)
    upper = grad_g.astype(bf16)
    lower = (grad_g - upper.astype(f32)).astype(bf16)
    spare = jnp.concatenate([upper, lower], axis=0)
    spare = jnp.pad(spare, ((0, 0), (0, 2 * half - d))).reshape(4, half)
    spare = jnp.broadcast_to(spare[None], (nz, 4, half))
    total_in = total_in.reshape(nz, PAD, half)[:, : 2 * rows].astype(bf16)
    total_in = lax.all_to_all(jnp.concatenate([total_in, spare], axis=1), "z", 0, 0)
    total_in = jnp.sum(total_in.astype(f32), axis=0)
    gain_rows = total_in[2 * rows : 2 * rows + 2] + total_in[2 * rows + 2 :]
    grad_inw, gain_other = returned(total_in[: 2 * rows], gain_rows)
    grad_g = (gain_rows + gain_other).reshape(1, 2 * half)[:, :d]
    return handed[None], grad_inw[None], grad_out[None], grad_g


def solution(mesh):
    nz, nx = 8, mesh.shape["dp"] // 16
    fine = Mesh(mesh.devices.reshape(nz, nx, 2, 2, 2), ("z", "x", "y", "h", "c"))
    wide = P(("h", "c"), ("z", "x", "y"), None)
    slim = P(("h", "c"), None)

    def run(*args):
        return local(nz, nx, *args)

    return jax.shard_map(
        run,
        mesh=fine,
        in_specs=(wide, wide, slim, wide, wide),
        out_specs=(wide, wide, wide, slim),
        check_vma=False,
    )
```

```python
import jax
import jax.numpy as jnp
from jax import lax
from jax.experimental import pallas as pl
from jax.experimental.pallas import tpu as pltpu
from jax.sharding import Mesh, PartitionSpec as P

coef = 0.7978845608
f32, bf16 = jnp.float32, jnp.bfloat16

SLOTS = (0, 1, 3, 2)
PAD = 40
COST = 200
VMEM = pltpu.CompilerParams(vmem_limit_bytes=56 * 1024 * 1024)


def shift(block, axis, distance):
    size = lax.axis_size(axis)
    return lax.ppermute(block, axis, [(i, (i + distance) % size) for i in range(size)])


def pick(flag, a, b):
    return jnp.where(flag == 0, a, b), jnp.where(flag == 0, b, a)


def ring_gather(block, axis):
    size, r = lax.axis_size(axis), block.shape[0]
    me = lax.axis_index(axis)
    out = jnp.zeros((size * r, block.shape[1]), block.dtype)
    out = lax.dynamic_update_slice(out, block, (me * r, 0))
    right = left = block
    for k in range(1, size // 2 + 1):
        right = shift(right, axis, 1)
        out = lax.dynamic_update_slice(out, right, ((me - k) % size * r, 0))
        if k < size - k:
            left = shift(left, axis, -1)
            out = lax.dynamic_update_slice(out, left, ((me + k) % size * r, 0))
    return out


def direct_gather(block, axis):
    size = lax.axis_size(axis)
    me = lax.axis_index(axis)
    out = jnp.zeros((size,) + block.shape, block.dtype)
    out = lax.dynamic_update_index_in_dim(out, block, me, 0)
    for k in range(1, size):
        got = shift(block, axis, k)
        out = lax.dynamic_update_index_in_dim(out, got, (me - k) % size, 0)
    return out


def dot(a, b, ca=1, cb=0):
    return lax.dot_general(a, b, (((ca,), (cb,)), ((), ())), preferred_element_type=f32)


def tiles(width):
    starts = list(range(0, width - 255, 256))
    ends = starts[1:] + [width]
    return list(zip(starts, ends))


def up_kernel(scaled, grads_t, first, slope, out_term, held, slopes, terms, sem):
    cuts = tiles(first.shape[1])
    loads, stores = [], []
    for i, (a, b) in enumerate(cuts):
        at = (slice(None), pl.ds(a, b - a))
        loads.append(pltpu.make_async_copy(first.at[at], held.at[at], sem.at[0, i]))
        stores.append(
            (
                pltpu.make_async_copy(slopes.at[at], slope.at[at], sem.at[1, i]),
                pltpu.make_async_copy(terms.at[at], out_term.at[at], sem.at[2, i]),
            )
        )
        loads[-1].start()
    for (a, b), load, (keep, send) in zip(cuts, loads, stores):
        load.wait()
        pre = dot(scaled[...], held[:, a:b])
        th = jnp.tanh(coef * (pre + 0.044715 * pre * pre * pre))
        slopes[:, a:b] = 0.5 * (1.0 + th) + 0.5 * pre * (1.0 - th * th) * coef * (
            1.0 + 0.134145 * pre * pre
        )
        keep.start()
        hidden = (0.5 * pre * (1.0 + th)).astype(bf16)
        terms[:, a:b] = dot(grads_t[...], hidden).astype(bf16)
        send.start()
    for pair in stores:
        for copy in pair:
            copy.wait()


def down_kernel(
    place, scale, grads, scaled_t, s0, s1, s2, s3, slope, first, normed,
    o0, o1, o2, o3, own, other, second, slopes, weights, plain, parts, terms, sem,
):
    rows, half = s0.shape
    t, d = plain.shape
    ins, outs = (s0, s1, s2, s3), (o0, o1, o2, o3)
    starts = [pl.multiple_of(place[0, j] * rows, rows) for j in range(4)]
    cuts = tiles(half)
    loads, stores = [], []
    for i, (a, b) in enumerate(cuts):
        cols = pl.ds(a, b - a)
        at = (slice(None), cols)
        load = [pltpu.make_async_copy(slope.at[at], slopes.at[at], sem.at[4, i])]
        store = []
        for j, start in enumerate(starts):
            block = (pl.ds(start, rows), cols)
            load.append(
                pltpu.make_async_copy(ins[j].at[at], second.at[block], sem.at[j, i])
            )
            piece = (pl.ds(j * rows, rows), cols)
            store.append(
                pltpu.make_async_copy(terms.at[piece], outs[j].at[at], sem.at[5 + j, i])
            )
        for copy in load:
            copy.start()
        loads.append(load)
        stores.append(store)
    late = [
        pltpu.make_async_copy(first, weights, sem.at[9, 0]),
        pltpu.make_async_copy(normed, plain, sem.at[9, 1]),
    ]
    for copy in late:
        copy.start()
    for (a, b), load in zip(cuts, loads):
        for copy in load:
            copy.wait()
        parts[:t, a:b] = (dot(grads[...], second[:, a:b]) * slopes[:, a:b]).astype(bf16)
    for copy in late:
        copy.wait()
    third = d // 3
    line = lax.broadcasted_iota(jnp.int32, (16, third), 0)
    spare = jnp.zeros((16, third), f32)
    for j in range(3):
        cols = slice(j * third, (j + 1) * third)
        back = dot(parts[:t], weights[cols], 1, 1)
        own[:, cols] = back[: t // 2]
        other[:, cols] = back[t // 2 :].astype(bf16)
        sums = jnp.sum(back * plain[:, cols], axis=0, keepdims=True) * scale[0, 0]
        spare = jnp.where(line == j, jnp.broadcast_to(sums, (16, third)), spare)
    parts[t:] = jnp.zeros((16, half), bf16)
    parts[t:, :third] = spare.astype(bf16)
    for (a, b), store in zip(cuts, stores):
        for j, start in enumerate(starts):
            terms[j * rows : (j + 1) * rows, a:b] = dot(
                scaled_t[pl.ds(start, rows)], parts[:, a:b]
            ).astype(bf16)
        for copy in store:
            copy.start()
    for store in stores:
        for copy in store:
            copy.wait()


WHOLE = pl.BlockSpec(memory_space=pltpu.VMEM)
AWAY = pl.BlockSpec(memory_space=pl.ANY)


def up(scaled, grads_t, first):
    t, d = scaled.shape
    half = first.shape[1]
    return pl.pallas_call(
        up_kernel,
        out_shape=(
            jax.ShapeDtypeStruct((t, half), f32),
            jax.ShapeDtypeStruct((d, half), bf16),
        ),
        in_specs=(WHOLE, WHOLE, AWAY),
        out_specs=(AWAY, AWAY),
        scratch_shapes=[
            pltpu.VMEM((d, half), bf16),
            pltpu.VMEM((t, half), f32),
            pltpu.VMEM((d, half), bf16),
            pltpu.SemaphoreType.DMA((3, len(tiles(half)))),
        ],
        compiler_params=VMEM,
        cost_estimate=pl.CostEstimate(
            flops=4 * t * d * half, bytes_accessed=4 * d * half, transcendentals=t * half
        ),
    )(scaled, grads_t, first)


def down(place, scale, grads, scaled_t, slots, slope, first, normed):
    t, wide = grads.shape
    rows, half = slots[0].shape
    d = first.shape[0]
    small = pl.BlockSpec(memory_space=pltpu.SMEM)
    return pl.pallas_call(
        down_kernel,
        out_shape=(jax.ShapeDtypeStruct((rows, half), bf16),) * 4
        + (
            jax.ShapeDtypeStruct((t // 2, d), f32),
            jax.ShapeDtypeStruct((t // 2, d), bf16),
        ),
        in_specs=[small, small, WHOLE, WHOLE] + [AWAY] * 7,
        out_specs=(AWAY,) * 4 + (WHOLE,) * 2,
        scratch_shapes=[
            pltpu.VMEM((wide, half), bf16),
            pltpu.VMEM((t, half), f32),
            pltpu.VMEM((d, half), bf16),
            pltpu.VMEM((t, d), f32),
            pltpu.VMEM((t + 16, half), bf16),
            pltpu.VMEM((wide, half), bf16),
            pltpu.SemaphoreType.DMA((10, len(tiles(half)))),
        ],
        compiler_params=VMEM,
        cost_estimate=pl.CostEstimate(
            flops=COST * t * wide * half, bytes_accessed=4 * wide * half, transcendentals=0
        ),
    )(place, scale, grads, scaled_t, *slots, slope, first, normed)


def selector(d, nz, nx):
    rows = d // (nz * nx)
    at = jnp.arange(nx * nz * PAD)
    block, line = at // PAD, at % PAD
    home = (block % nz * nx + block // nz) * rows + line
    home = jnp.where(line < rows, home, -1)
    return (jnp.arange(d)[:, None] == home[None]).astype(bf16)


def after(value, *others):
    return lax.optimization_barrier((value,) + others)[0]


def local(nz, nx, acts, grad_in, gain, w_in, w_out):
    x, y = lax.axis_index("x"), lax.axis_index("y")
    rows, hid = w_in.shape[1:]
    half = hid // 2
    tokens, d = acts.shape[1:]
    scale = 1.0 / jnp.sqrt(jnp.float32(tokens * nz * nx * 2))

    both = jnp.concatenate([w_in, w_out], axis=0)
    mine, theirs = pick(y, both[:, :, :half], both[:, :, half:])
    top, bottom = pick(y, mine, shift(theirs, "y", 1))
    shard = jnp.concatenate([top, bottom], axis=1)
    first = direct_gather(shard[0], "x").reshape(nx * 2 * rows, half)
    first = lax.all_gather(first, "z", axis=0, tiled=True)
    second = ring_gather(jnp.pad(shard[1], ((0, PAD - 2 * rows), (0, 0))), "z")
    slots = [second] + [shift(second, "x", -o) for o in SLOTS[1:]]

    source = jnp.concatenate([acts[0], shift(acts[0], "y", 1)], axis=0).astype(f32)
    centred = source - jnp.mean(source, axis=1, keepdims=True)
    inv = 1.0 / jnp.sqrt(jnp.mean(centred * centred, axis=1, keepdims=True) + 1e-06)
    normed = centred * inv
    scaled = (normed * gain[0][None, :]).astype(bf16)
    grads = jnp.concatenate([grad_in[0], shift(grad_in[0], "y", 1)], axis=0)
    chosen = selector(d, nz, nx)
    scaled_t = dot(chosen, scaled, 0, 1).astype(bf16)
    at = jnp.arange(nx * nz * PAD)[:, None] % PAD - 2 * rows
    spots = (at == jnp.arange(16)[None]) & (at < 3)
    scaled_t = jnp.concatenate([scaled_t, spots.astype(bf16)], axis=1)
    grads_w = dot(grads, chosen).astype(bf16)

    scaled, first, grads_t = lax.optimization_barrier(
        (scaled, first, grads.T, second, scaled_t, grads_w)
    )[:3]
    slope, out_term = up(scaled, grads_t, first)
    sum_out = lax.psum_scatter(out_term, "z", scatter_dimension=0, tiled=True)
    sum_out = sum_out.reshape(nx, 2 * rows, half)
    total_out = lax.dynamic_index_in_dim(sum_out, x, 0, keepdims=False).astype(f32)
    for o in SLOTS[1:]:
        part = lax.dynamic_index_in_dim(sum_out, (x + o) % nx, 0, keepdims=False)
        total_out += shift(part, "x", o).astype(f32)

    def returned(total, extra):
        total = total * scale
        keep, send = pick(y, total[:rows], total[rows:])
        if extra is not None:
            send = jnp.concatenate([send, extra], axis=0)
        got = shift(send, "y", 1)
        low, high = pick(y, keep, got[:rows])
        return jnp.concatenate([low, high], axis=1), got[rows:]

    grad_out, _ = returned(total_out, None)

    place = jnp.stack([(x + o) % nx for o in SLOTS]).astype(jnp.int32)[None]
    *terms, own, other = down(
        place, scale.reshape(1, 1), grads_w, scaled_t, slots, slope, first, normed
    )
    total_in = terms[0].astype(f32)
    for o, term in zip(SLOTS[1:], terms[1:]):
        total_in += shift(term, "x", o).astype(f32)

    dscaled = own + shift(other, "y", 1).astype(f32)
    dnormed = dscaled * gain[0][None, :]
    normed, inv = normed[:tokens], inv[:tokens]
    grad_x = grad_in[0].astype(f32) + inv * (
        dnormed
        - jnp.mean(dnormed, axis=1, keepdims=True)
        - normed * jnp.mean(dnormed * normed, axis=1, keepdims=True)
    )
    route = [(2 * h + c, (2 * h + c - 1) % 4) for h in range(2) for c in range(2)]
    handed = lax.ppermute(grad_x.astype(bf16), ("h", "c"), route)

    total_in = after(total_in.astype(bf16), sum_out).reshape(nz, PAD, half)
    total_in = lax.all_to_all(total_in, "z", 0, 0)
    total_in = jnp.sum(total_in.astype(f32), axis=0)
    gain_rows = total_in[2 * rows : 2 * rows + 3]
    grad_inw, gain_other = returned(total_in[: 2 * rows], gain_rows)
    grad_g = (gain_rows + gain_other)[:, : d // 3].reshape(1, d)
    return handed[None], grad_inw[None], grad_out[None], grad_g


def solution(mesh):
    nz, nx = 8, mesh.shape["dp"] // 16
    fine = Mesh(mesh.devices.reshape(nz, nx, 2, 2, 2), ("z", "x", "y", "h", "c"))
    wide = P(("h", "c"), ("z", "x", "y"), None)
    slim = P(("h", "c"), None)

    def run(*args):
        return local(nz, nx, *args)

    return jax.shard_map(
        run,
        mesh=fine,
        in_specs=(wide, wide, slim, wide, wide),
        out_specs=(wide, wide, wide, slim),
        check_vma=False,
    )
```

```python
import jax
import jax.numpy as jnp
from jax import lax
from jax.experimental import pallas as pl
from jax.experimental.pallas import tpu as pltpu
from jax.sharding import Mesh, PartitionSpec as P

coef = 0.7978845608
f32, bf16 = jnp.float32, jnp.bfloat16

SLOTS = (0, 1, 3, 2)
PAD = 40
COST = 200
VMEM = pltpu.CompilerParams(vmem_limit_bytes=56 * 1024 * 1024)


def shift(block, axis, distance):
    size = lax.axis_size(axis)
    return lax.ppermute(block, axis, [(i, (i + distance) % size) for i in range(size)])


def pick(flag, a, b):
    return jnp.where(flag == 0, a, b), jnp.where(flag == 0, b, a)


def ring_gather(block, first, axis, beside):
    size, r = lax.axis_size(axis), block.shape[0]
    me = lax.axis_index(axis)
    out = jnp.zeros((size * r, block.shape[1]), block.dtype)
    out = lax.dynamic_update_slice(out, block, (me * r, 0))
    right, left = first
    for k in range(1, size // 2 + 1):
        if k > 1:
            right, left = after(right, *beside[k - 2]), after(left, *beside[k - 2])
            right, left = shift(right, axis, 1), shift(left, axis, -1)
        out = lax.dynamic_update_slice(out, right, ((me - k) % size * r, 0))
        if k < size - k:
            out = lax.dynamic_update_slice(out, left, ((me + k) % size * r, 0))
    return out


def after(value, *others):
    return lax.optimization_barrier((value,) + others)[0]


def direct_gather(block, axis):
    size = lax.axis_size(axis)
    me = lax.axis_index(axis)
    out = jnp.zeros((size,) + block.shape, block.dtype)
    out = lax.dynamic_update_index_in_dim(out, block, me, 0)
    for k in range(1, size):
        got = shift(block, axis, k)
        out = lax.dynamic_update_index_in_dim(out, got, (me - k) % size, 0)
    return out


def dot(a, b, ca=1, cb=0):
    return lax.dot_general(a, b, (((ca,), (cb,)), ((), ())), preferred_element_type=f32)


def tiles(width):
    starts = list(range(0, width - 255, 256))
    ends = starts[1:] + [width]
    return list(zip(starts, ends))


def up_kernel(scaled, grads_t, first, slope, out_term, held, slopes, terms, sem):
    cuts = tiles(first.shape[1])
    loads, stores = [], []
    for i, (a, b) in enumerate(cuts):
        at = (slice(None), pl.ds(a, b - a))
        loads.append(pltpu.make_async_copy(first.at[at], held.at[at], sem.at[0, i]))
        stores.append(
            (
                pltpu.make_async_copy(slopes.at[at], slope.at[at], sem.at[1, i]),
                pltpu.make_async_copy(terms.at[at], out_term.at[at], sem.at[2, i]),
            )
        )
        loads[-1].start()
    for (a, b), load, (keep, send) in zip(cuts, loads, stores):
        load.wait()
        pre = dot(scaled[...], held[:, a:b])
        th = jnp.tanh(coef * (pre + 0.044715 * pre * pre * pre))
        slopes[:, a:b] = 0.5 * (1.0 + th) + 0.5 * pre * (1.0 - th * th) * coef * (
            1.0 + 0.134145 * pre * pre
        )
        keep.start()
        hidden = (0.5 * pre * (1.0 + th)).astype(bf16)
        terms[:, a:b] = dot(grads_t[...], hidden).astype(bf16)
        send.start()
    for pair in stores:
        for copy in pair:
            copy.wait()


def down_kernel(
    place, scale, grads, scaled_t, s0, s1, s2, s3, slope, first, normed,
    o0, o1, o2, o3, own, other, second, slopes, weights, plain, parts, terms, sem,
):
    rows, half = s0.shape
    t, d = plain.shape
    ins, outs = (s0, s1, s2, s3), (o0, o1, o2, o3)
    starts = [pl.multiple_of(place[0, j] * rows, rows) for j in range(4)]
    cuts = tiles(half)
    loads, stores = [], []
    for i, (a, b) in enumerate(cuts):
        cols = pl.ds(a, b - a)
        at = (slice(None), cols)
        load = [pltpu.make_async_copy(slope.at[at], slopes.at[at], sem.at[4, i])]
        store = []
        for j, start in enumerate(starts):
            block = (pl.ds(start, rows), cols)
            load.append(
                pltpu.make_async_copy(ins[j].at[at], second.at[block], sem.at[j, i])
            )
            piece = (pl.ds(j * rows, rows), cols)
            store.append(
                pltpu.make_async_copy(terms.at[piece], outs[j].at[at], sem.at[5 + j, i])
            )
        for copy in load:
            copy.start()
        loads.append(load)
        stores.append(store)
    late = [
        pltpu.make_async_copy(first, weights, sem.at[9, 0]),
        pltpu.make_async_copy(normed, plain, sem.at[9, 1]),
    ]
    for copy in late:
        copy.start()
    for (a, b), load in zip(cuts, loads):
        for copy in load:
            copy.wait()
        parts[:t, a:b] = (dot(grads[...], second[:, a:b]) * slopes[:, a:b]).astype(bf16)
    for copy in late:
        copy.wait()
    third = d // 3
    line = lax.broadcasted_iota(jnp.int32, (16, third), 0)
    spare = jnp.zeros((16, third), f32)
    for j in range(3):
        cols = slice(j * third, (j + 1) * third)
        back = dot(parts[:t], weights[cols], 1, 1)
        own[:, cols] = back[: t // 2]
        other[:, cols] = back[t // 2 :].astype(bf16)
        sums = jnp.sum(back * plain[:, cols], axis=0, keepdims=True) * scale[0, 0]
        spare = jnp.where(line == j, jnp.broadcast_to(sums, (16, third)), spare)
    parts[t:] = jnp.zeros((16, half), bf16)
    parts[t:, :third] = spare.astype(bf16)
    for (a, b), store in zip(cuts, stores):
        for j, start in enumerate(starts):
            terms[j * rows : (j + 1) * rows, a:b] = dot(
                scaled_t[pl.ds(start, rows)], parts[:, a:b]
            ).astype(bf16)
        for copy in store:
            copy.start()
    for store in stores:
        for copy in store:
            copy.wait()


WHOLE = pl.BlockSpec(memory_space=pltpu.VMEM)
AWAY = pl.BlockSpec(memory_space=pl.ANY)


def up(scaled, grads_t, first):
    t, d = scaled.shape
    half = first.shape[1]
    return pl.pallas_call(
        up_kernel,
        out_shape=(
            jax.ShapeDtypeStruct((t, half), f32),
            jax.ShapeDtypeStruct((d, half), bf16),
        ),
        in_specs=(WHOLE, WHOLE, AWAY),
        out_specs=(AWAY, AWAY),
        scratch_shapes=[
            pltpu.VMEM((d, half), bf16),
            pltpu.VMEM((t, half), f32),
            pltpu.VMEM((d, half), bf16),
            pltpu.SemaphoreType.DMA((3, len(tiles(half)))),
        ],
        compiler_params=VMEM,
        cost_estimate=pl.CostEstimate(
            flops=4 * t * d * half, bytes_accessed=4 * d * half, transcendentals=t * half
        ),
    )(scaled, grads_t, first)


def down(place, scale, grads, scaled_t, slots, slope, first, normed):
    t, wide = grads.shape
    rows, half = slots[0].shape
    d = first.shape[0]
    small = pl.BlockSpec(memory_space=pltpu.SMEM)
    return pl.pallas_call(
        down_kernel,
        out_shape=(jax.ShapeDtypeStruct((rows, half), bf16),) * 4
        + (
            jax.ShapeDtypeStruct((t // 2, d), f32),
            jax.ShapeDtypeStruct((t // 2, d), bf16),
        ),
        in_specs=[small, small, WHOLE, WHOLE] + [AWAY] * 7,
        out_specs=(AWAY,) * 4 + (WHOLE,) * 2,
        scratch_shapes=[
            pltpu.VMEM((wide, half), bf16),
            pltpu.VMEM((t, half), f32),
            pltpu.VMEM((d, half), bf16),
            pltpu.VMEM((t, d), f32),
            pltpu.VMEM((t + 16, half), bf16),
            pltpu.VMEM((wide, half), bf16),
            pltpu.SemaphoreType.DMA((10, len(tiles(half)))),
        ],
        compiler_params=VMEM,
        cost_estimate=pl.CostEstimate(
            flops=COST * t * wide * half, bytes_accessed=4 * wide * half, transcendentals=0
        ),
    )(place, scale, grads, scaled_t, *slots, slope, first, normed)


def selector(d, nz, nx):
    rows = d // (nz * nx)
    at = jnp.arange(nx * nz * PAD)
    block, line = at // PAD, at % PAD
    home = (block % nz * nx + block // nz) * rows + line
    home = jnp.where(line < rows, home, -1)
    return (jnp.arange(d)[:, None] == home[None]).astype(bf16)


def local(nz, nx, acts, grad_in, gain, w_in, w_out):
    x, y = lax.axis_index("x"), lax.axis_index("y")
    rows, hid = w_in.shape[1:]
    half = hid // 2
    tokens, d = acts.shape[1:]
    scale = 1.0 / jnp.sqrt(jnp.float32(tokens * nz * nx * 2))

    shards = []
    for w in (w_in[0], w_out[0]):
        mine, theirs = pick(y, w[:, :half], w[:, half:])
        top, bottom = pick(y, mine, shift(theirs, "y", 1))
        shards.append(jnp.concatenate([top, bottom], axis=0))
    block = jnp.pad(shards[1], ((0, PAD - 2 * rows), (0, 0)))
    step = shift(block, "z", 1), shift(block, "z", -1)
    first = direct_gather(shards[0], "x").reshape(nx * 2 * rows, half)
    first = lax.all_gather(after(first, *step), "z", axis=0, tiled=True)

    source = jnp.concatenate([acts[0], shift(acts[0], "y", 1)], axis=0).astype(f32)
    centred = source - jnp.mean(source, axis=1, keepdims=True)
    inv = 1.0 / jnp.sqrt(jnp.mean(centred * centred, axis=1, keepdims=True) + 1e-06)
    normed = centred * inv
    scaled = (normed * gain[0][None, :]).astype(bf16)
    grads = jnp.concatenate([grad_in[0], shift(grad_in[0], "y", 1)], axis=0)
    chosen = selector(d, nz, nx)
    scaled_t = dot(chosen, scaled, 0, 1).astype(bf16)
    at = jnp.arange(nx * nz * PAD)[:, None] % PAD - 2 * rows
    spots = (at == jnp.arange(16)[None]) & (at < 3)
    scaled_t = jnp.concatenate([scaled_t, spots.astype(bf16)], axis=1)
    grads_w = dot(grads, chosen).astype(bf16)

    second = ring_gather(block, step, "z", [(), (scaled,), (scaled_t, grads_w)])
    slots = [second] + [shift(second, "x", -o) for o in SLOTS[1:]]
    scaled, first, grads_t = lax.optimization_barrier(
        (scaled, first, grads.T, second, scaled_t, grads_w)
    )[:3]
    slope, out_term = up(scaled, grads_t, first)
    sum_out = lax.psum_scatter(out_term, "z", scatter_dimension=0, tiled=True)
    place = jnp.stack([(x + o) % nx for o in SLOTS]).astype(jnp.int32)[None]
    *terms, own, other = down(
        place, scale.reshape(1, 1), grads_w, scaled_t, slots, slope, first, normed
    )
    total_in = terms[0].astype(f32)
    for o, term in zip(SLOTS[1:], terms[1:]):
        total_in += shift(term, "x", o).astype(f32)
    sum_out, total_in = lax.optimization_barrier((sum_out, total_in.astype(bf16)))

    sum_out = sum_out.reshape(nx, 2 * rows, half)
    total_out = lax.dynamic_index_in_dim(sum_out, x, 0, keepdims=False).astype(f32)
    for o in SLOTS[1:]:
        part = lax.dynamic_index_in_dim(sum_out, (x + o) % nx, 0, keepdims=False)
        total_out += shift(part, "x", o).astype(f32)

    dscaled = own + shift(other, "y", 1).astype(f32)
    dnormed = dscaled * gain[0][None, :]
    normed, inv = normed[:tokens], inv[:tokens]
    grad_x = grad_in[0].astype(f32) + inv * (
        dnormed
        - jnp.mean(dnormed, axis=1, keepdims=True)
        - normed * jnp.mean(dnormed * normed, axis=1, keepdims=True)
    )
    route = [(2 * h + c, (2 * h + c - 1) % 4) for h in range(2) for c in range(2)]
    handed = lax.ppermute(grad_x.astype(bf16), ("h", "c"), route)

    total_in = lax.all_to_all(total_in.reshape(nz, PAD, half), "z", 0, 0)
    total_in = jnp.sum(total_in.astype(f32), axis=0)
    gain_rows = total_in[2 * rows : 2 * rows + 3]

    keeps, sends = zip(
        *(pick(y, w[:rows], w[rows : 2 * rows]) for w in (total_in * scale, total_out * scale))
    )
    got = shift(jnp.concatenate(sends + (gain_rows,), axis=0), "y", 1)
    grad_inw, grad_out = (
        jnp.concatenate(pick(y, keep, got[rows * i : rows * (i + 1)]), axis=1)
        for i, keep in enumerate(keeps)
    )
    grad_g = (gain_rows + got[2 * rows :])[:, : d // 3].reshape(1, d)
    return handed[None], grad_inw[None], grad_out[None], grad_g


def solution(mesh):
    nz, nx = 8, mesh.shape["dp"] // 16
    fine = Mesh(mesh.devices.reshape(nz, nx, 2, 2, 2), ("z", "x", "y", "h", "c"))
    wide = P(("h", "c"), ("z", "x", "y"), None)
    slim = P(("h", "c"), None)

    def run(*args):
        return local(nz, nx, *args)

    return jax.shard_map(
        run,
        mesh=fine,
        in_specs=(wide, wide, slim, wide, wide),
        out_specs=(wide, wide, wide, slim),
        check_vma=False,
    )
```

```python
import jax
import jax.numpy as jnp
from jax import lax
from jax.experimental import pallas as pl
from jax.experimental.pallas import tpu as pltpu
from jax.sharding import Mesh, PartitionSpec as P

coef = 0.7978845608
f32, bf16 = jnp.float32, jnp.bfloat16

SLOTS = (0, 1, 3, 2)
PAD = 40
COST = 200
VMEM = pltpu.CompilerParams(vmem_limit_bytes=56 * 1024 * 1024)


def shift(block, axis, distance):
    size = lax.axis_size(axis)
    return lax.ppermute(block, axis, [(i, (i + distance) % size) for i in range(size)])


def pick(flag, a, b):
    return jnp.where(flag == 0, a, b), jnp.where(flag == 0, b, a)


def ring_gather(block, first, axis, beside):
    size, r = lax.axis_size(axis), block.shape[0]
    me = lax.axis_index(axis)
    out = jnp.zeros((size * r, block.shape[1]), block.dtype)
    out = lax.dynamic_update_slice(out, block, (me * r, 0))
    right, left = first
    for k in range(1, size // 2 + 1):
        if k > 1:
            right, left = after(right, *beside[k - 2]), after(left, *beside[k - 2])
            right, left = shift(right, axis, 1), shift(left, axis, -1)
        out = lax.dynamic_update_slice(out, right, ((me - k) % size * r, 0))
        if k < size - k:
            out = lax.dynamic_update_slice(out, left, ((me + k) % size * r, 0))
    return out


def after(value, *others):
    return lax.optimization_barrier((value,) + others)[0]


def direct_gather(block, axis):
    size = lax.axis_size(axis)
    me = lax.axis_index(axis)
    out = jnp.zeros((size,) + block.shape, block.dtype)
    out = lax.dynamic_update_index_in_dim(out, block, me, 0)
    for k in range(1, size):
        got = shift(block, axis, k)
        out = lax.dynamic_update_index_in_dim(out, got, (me - k) % size, 0)
    return out


def dot(a, b, ca=1, cb=0):
    return lax.dot_general(a, b, (((ca,), (cb,)), ((), ())), preferred_element_type=f32)


def tiles(width):
    starts = list(range(0, width - 255, 256))
    ends = starts[1:] + [width]
    return list(zip(starts, ends))


def up_kernel(scaled, grads_t, first, slope, out_term, held, slopes, terms, sem):
    cuts = tiles(first.shape[1])
    loads, stores = [], []
    for i, (a, b) in enumerate(cuts):
        at = (slice(None), pl.ds(a, b - a))
        loads.append(pltpu.make_async_copy(first.at[at], held.at[at], sem.at[0, i]))
        stores.append(
            (
                pltpu.make_async_copy(slopes.at[at], slope.at[at], sem.at[1, i]),
                pltpu.make_async_copy(terms.at[at], out_term.at[at], sem.at[2, i]),
            )
        )
        loads[-1].start()
    for (a, b), load, (keep, send) in zip(cuts, loads, stores):
        load.wait()
        pre = dot(scaled[...], held[:, a:b])
        th = jnp.tanh(coef * (pre + 0.044715 * pre * pre * pre))
        slopes[:, a:b] = 0.5 * (1.0 + th) + 0.5 * pre * (1.0 - th * th) * coef * (
            1.0 + 0.134145 * pre * pre
        )
        keep.start()
        hidden = (0.5 * pre * (1.0 + th)).astype(bf16)
        terms[:, a:b] = dot(grads_t[...], hidden).astype(bf16)
        send.start()
    for pair in stores:
        for copy in pair:
            copy.wait()


def down_kernel(
    place, ratio, grads, scaled_t, s0, s1, s2, s3, slope, first, scaled,
    o0, o1, o2, o3, own, other, second, slopes, weights, plain, parts, terms, sem,
):
    rows, half = s0.shape
    t, d = plain.shape
    ins, outs = (s0, s1, s2, s3), (o0, o1, o2, o3)
    starts = [pl.multiple_of(place[0, j] * rows, rows) for j in range(4)]
    cuts = tiles(half)
    loads, stores = [], []
    for i, (a, b) in enumerate(cuts):
        cols = pl.ds(a, b - a)
        at = (slice(None), cols)
        load = [pltpu.make_async_copy(slope.at[at], slopes.at[at], sem.at[4, i])]
        store = []
        for j, start in enumerate(starts):
            block = (pl.ds(start, rows), cols)
            load.append(
                pltpu.make_async_copy(ins[j].at[at], second.at[block], sem.at[j, i])
            )
            piece = (pl.ds(j * rows, rows), cols)
            store.append(
                pltpu.make_async_copy(terms.at[piece], outs[j].at[at], sem.at[5 + j, i])
            )
        for copy in load:
            copy.start()
        loads.append(load)
        stores.append(store)
    late = [
        pltpu.make_async_copy(first, weights, sem.at[9, 0]),
        pltpu.make_async_copy(scaled, plain, sem.at[9, 1]),
    ]
    for copy in late:
        copy.start()
    for (a, b), load in zip(cuts, loads):
        for copy in load:
            copy.wait()
        parts[:t, a:b] = (dot(grads[...], second[:, a:b]) * slopes[:, a:b]).astype(bf16)
    for copy in late:
        copy.wait()
    third = d // 3
    line = lax.broadcasted_iota(jnp.int32, (16, third), 0)
    spare = jnp.zeros((16, third), f32)
    for j in range(3):
        cols = slice(j * third, (j + 1) * third)
        back = dot(parts[:t], weights[cols], 1, 1)
        own[:, cols] = back[: t // 2]
        other[:, cols] = back[t // 2 :].astype(bf16)
        sums = jnp.sum(back * plain[:, cols].astype(f32), axis=0, keepdims=True)
        sums *= ratio[:, cols]
        spare = jnp.where(line == j, jnp.broadcast_to(sums, (16, third)), spare)
    parts[t:] = jnp.zeros((16, half), bf16)
    parts[t:, :third] = spare.astype(bf16)
    for (a, b), store in zip(cuts, stores):
        for j, start in enumerate(starts):
            terms[j * rows : (j + 1) * rows, a:b] = dot(
                scaled_t[pl.ds(start, rows)], parts[:, a:b]
            ).astype(bf16)
        for copy in store:
            copy.start()
    for store in stores:
        for copy in store:
            copy.wait()


WHOLE = pl.BlockSpec(memory_space=pltpu.VMEM)
AWAY = pl.BlockSpec(memory_space=pl.ANY)


def up(scaled, grads_t, first):
    t, d = scaled.shape
    half = first.shape[1]
    return pl.pallas_call(
        up_kernel,
        out_shape=(
            jax.ShapeDtypeStruct((t, half), f32),
            jax.ShapeDtypeStruct((d, half), bf16),
        ),
        in_specs=(WHOLE, WHOLE, AWAY),
        out_specs=(AWAY, AWAY),
        scratch_shapes=[
            pltpu.VMEM((d, half), bf16),
            pltpu.VMEM((t, half), f32),
            pltpu.VMEM((d, half), bf16),
            pltpu.SemaphoreType.DMA((3, len(tiles(half)))),
        ],
        compiler_params=VMEM,
        cost_estimate=pl.CostEstimate(
            flops=4 * t * d * half, bytes_accessed=4 * d * half, transcendentals=t * half
        ),
    )(scaled, grads_t, first)


def down(place, ratio, grads, scaled_t, slots, slope, first, scaled):
    t, wide = grads.shape
    rows, half = slots[0].shape
    d = first.shape[0]
    small = pl.BlockSpec(memory_space=pltpu.SMEM)
    return pl.pallas_call(
        down_kernel,
        out_shape=(jax.ShapeDtypeStruct((rows, half), bf16),) * 4
        + (
            jax.ShapeDtypeStruct((t // 2, d), f32),
            jax.ShapeDtypeStruct((t // 2, d), bf16),
        ),
        in_specs=[small, WHOLE, WHOLE, WHOLE] + [AWAY] * 7,
        out_specs=(AWAY,) * 4 + (WHOLE,) * 2,
        scratch_shapes=[
            pltpu.VMEM((wide, half), bf16),
            pltpu.VMEM((t, half), f32),
            pltpu.VMEM((d, half), bf16),
            pltpu.VMEM((t, d), bf16),
            pltpu.VMEM((t + 16, half), bf16),
            pltpu.VMEM((wide, half), bf16),
            pltpu.SemaphoreType.DMA((10, len(tiles(half)))),
        ],
        compiler_params=VMEM,
        cost_estimate=pl.CostEstimate(
            flops=COST * t * wide * half, bytes_accessed=4 * wide * half, transcendentals=0
        ),
    )(place, ratio, grads, scaled_t, *slots, slope, first, scaled)


def selector(d, nz, nx):
    rows = d // (nz * nx)
    at = jnp.arange(nx * nz * PAD)
    block, line = at // PAD, at % PAD
    home = (block % nz * nx + block // nz) * rows + line
    home = jnp.where(line < rows, home, -1)
    return (jnp.arange(d)[:, None] == home[None]).astype(bf16)


def local(nz, nx, acts, grad_in, gain, w_in, w_out):
    x, y = lax.axis_index("x"), lax.axis_index("y")
    rows, hid = w_in.shape[1:]
    half = hid // 2
    tokens, d = acts.shape[1:]
    scale = 1.0 / jnp.sqrt(jnp.float32(tokens * nz * nx * 2))

    shards = []
    for w in (w_in[0], w_out[0]):
        mine, theirs = pick(y, w[:, :half], w[:, half:])
        top, bottom = pick(y, mine, shift(theirs, "y", 1))
        shards.append(jnp.concatenate([top, bottom], axis=0))
    block = jnp.pad(shards[1], ((0, PAD - 2 * rows), (0, 0)))
    step = shift(block, "z", 1), shift(block, "z", -1)
    first = direct_gather(shards[0], "x").reshape(nx * 2 * rows, half)
    first = lax.all_gather(after(first, *step), "z", axis=0, tiled=True)

    source = acts[0].astype(f32)
    centred = source - jnp.mean(source, axis=1, keepdims=True)
    inv = 1.0 / jnp.sqrt(jnp.mean(centred * centred, axis=1, keepdims=True) + 1e-06)
    normed = centred * inv
    scaled = (normed * gain[0][None, :]).astype(bf16)
    scaled = jnp.concatenate([scaled, shift(scaled, "y", 1)], axis=0)
    grads = jnp.concatenate([grad_in[0], shift(grad_in[0], "y", 1)], axis=0)
    chosen = selector(d, nz, nx)
    scaled_t = dot(chosen, scaled, 0, 1).astype(bf16)
    at = jnp.arange(nx * nz * PAD)[:, None] % PAD - 2 * rows
    spots = (at == jnp.arange(16)[None]) & (at < 3)
    scaled_t = jnp.concatenate([scaled_t, spots.astype(bf16)], axis=1)
    grads_w = dot(grads, chosen).astype(bf16)

    second = ring_gather(block, step, "z", [(), (), ()])
    slots = [second] + [shift(second, "x", -o) for o in SLOTS[1:]]
    scaled, first, grads_t = lax.optimization_barrier(
        (scaled, first, grads.T, second, scaled_t, grads_w)
    )[:3]
    slope, out_term = up(scaled, grads_t, first)
    sum_out = lax.psum_scatter(out_term, "z", scatter_dimension=0, tiled=True)
    place = jnp.stack([(x + o) % nx for o in SLOTS]).astype(jnp.int32)[None]
    *terms, own, other = down(
        place, scale / gain, grads_w, scaled_t, slots, slope, first, scaled
    )
    total_in = terms[0].astype(f32)
    for o, term in zip(SLOTS[1:], terms[1:]):
        total_in += shift(term, "x", o).astype(f32)
    sum_out, total_in = lax.optimization_barrier((sum_out, total_in.astype(bf16)))

    sum_out = sum_out.reshape(nx, 2 * rows, half)
    total_out = lax.dynamic_index_in_dim(sum_out, x, 0, keepdims=False).astype(f32)
    for o in SLOTS[1:]:
        part = lax.dynamic_index_in_dim(sum_out, (x + o) % nx, 0, keepdims=False)
        total_out += shift(part, "x", o).astype(f32)

    dscaled = own + shift(other, "y", 1).astype(f32)
    dnormed = dscaled * gain[0][None, :]
    grad_x = grad_in[0].astype(f32) + inv * (
        dnormed
        - jnp.mean(dnormed, axis=1, keepdims=True)
        - normed * jnp.mean(dnormed * normed, axis=1, keepdims=True)
    )
    route = [(2 * h + c, (2 * h + c - 1) % 4) for h in range(2) for c in range(2)]
    handed = lax.ppermute(grad_x.astype(bf16), ("h", "c"), route)

    total_in = lax.all_to_all(total_in.reshape(nz, PAD, half), "z", 0, 0)
    total_in = jnp.sum(total_in.astype(f32), axis=0)
    gain_rows = total_in[2 * rows : 2 * rows + 3]

    keeps, sends = zip(
        *(pick(y, w[:rows], w[rows : 2 * rows]) for w in (total_in * scale, total_out * scale))
    )
    got = shift(jnp.concatenate(sends + (gain_rows,), axis=0), "y", 1)
    grad_inw, grad_out = (
        jnp.concatenate(pick(y, keep, got[rows * i : rows * (i + 1)]), axis=1)
        for i, keep in enumerate(keeps)
    )
    grad_g = (gain_rows + got[2 * rows :])[:, : d // 3].reshape(1, d)
    return handed[None], grad_inw[None], grad_out[None], grad_g


def solution(mesh):
    nz, nx = 8, mesh.shape["dp"] // 16
    fine = Mesh(mesh.devices.reshape(nz, nx, 2, 2, 2), ("z", "x", "y", "h", "c"))
    wide = P(("h", "c"), ("z", "x", "y"), None)
    slim = P(("h", "c"), None)

    def run(*args):
        return local(nz, nx, *args)

    return jax.shard_map(
        run,
        mesh=fine,
        in_specs=(wide, wide, slim, wide, wide),
        out_specs=(wide, wide, wide, slim),
        check_vma=False,
    )
```

```python
import jax
import jax.numpy as jnp
from jax import lax
from jax.experimental import pallas as pl
from jax.experimental.pallas import tpu as pltpu
from jax.sharding import Mesh, PartitionSpec as P

coef = 0.7978845608
f32, bf16 = jnp.float32, jnp.bfloat16

SLOTS = (0, 1, 3, 2)
PAD = 40
COST = 200
VMEM = pltpu.CompilerParams(vmem_limit_bytes=56 * 1024 * 1024)


def shift(block, axis, distance):
    size = lax.axis_size(axis)
    return lax.ppermute(block, axis, [(i, (i + distance) % size) for i in range(size)])


def pick(flag, a, b):
    return jnp.where(flag == 0, a, b), jnp.where(flag == 0, b, a)


def ring_gather(block, first, axis, beside):
    size, r = lax.axis_size(axis), block.shape[0]
    me = lax.axis_index(axis)
    out = jnp.zeros((size * r, block.shape[1]), block.dtype)
    out = lax.dynamic_update_slice(out, block, (me * r, 0))
    right, left = first
    for k in range(1, size // 2 + 1):
        if k > 1:
            right, left = after(right, *beside[k - 2]), after(left, *beside[k - 2])
            right, left = shift(right, axis, 1), shift(left, axis, -1)
        out = lax.dynamic_update_slice(out, right, ((me - k) % size * r, 0))
        if k < size - k:
            out = lax.dynamic_update_slice(out, left, ((me + k) % size * r, 0))
    return out


def after(value, *others):
    return lax.optimization_barrier((value,) + others)[0]


def direct_gather(block, axis):
    size = lax.axis_size(axis)
    me = lax.axis_index(axis)
    out = jnp.zeros((size,) + block.shape, block.dtype)
    out = lax.dynamic_update_index_in_dim(out, block, me, 0)
    for k in range(1, size):
        got = shift(block, axis, k)
        out = lax.dynamic_update_index_in_dim(out, got, (me - k) % size, 0)
    return out


def dot(a, b, ca=1, cb=0):
    return lax.dot_general(a, b, (((ca,), (cb,)), ((), ())), preferred_element_type=f32)


def tiles(width):
    starts = list(range(0, width - 255, 256))
    ends = starts[1:] + [width]
    return list(zip(starts, ends))


def up_kernel(scaled, grads_t, first, slope, out_term, held, slopes, terms, sem):
    cuts = tiles(first.shape[1])
    loads, stores = [], []
    for i, (a, b) in enumerate(cuts):
        at = (slice(None), pl.ds(a, b - a))
        loads.append(pltpu.make_async_copy(first.at[at], held.at[at], sem.at[0, i]))
        stores.append(
            (
                pltpu.make_async_copy(slopes.at[at], slope.at[at], sem.at[1, i]),
                pltpu.make_async_copy(terms.at[at], out_term.at[at], sem.at[2, i]),
            )
        )
        loads[-1].start()
    for (a, b), load, (keep, send) in zip(cuts, loads, stores):
        load.wait()
        pre = dot(scaled[...], held[:, a:b])
        square = pre * pre
        part = 0.5 + 0.5 * jnp.tanh(pre * (coef + (coef * 0.044715) * square))
        slopes[:, a:b] = part + part * (1.0 - part) * (
            pre * (2.0 * coef + (2.0 * coef * 0.134145) * square)
        )
        keep.start()
        hidden = (pre * part).astype(bf16)
        terms[:, a:b] = dot(grads_t[...], hidden).astype(bf16)
        send.start()
    for pair in stores:
        for copy in pair:
            copy.wait()


def down_kernel(
    place, grads, scaled_t, s0, s1, s2, s3, slope, dpre, o0, o1, o2, o3,
    second, slopes, parts, terms, sem,
):
    rows = s0.shape[0]
    ins, outs = (s0, s1, s2, s3), (o0, o1, o2, o3)
    starts = [pl.multiple_of(place[0, j] * rows, rows) for j in range(4)]
    cuts = tiles(second.shape[1])
    loads, stores = [], []
    for i, (a, b) in enumerate(cuts):
        cols = pl.ds(a, b - a)
        at = (slice(None), cols)
        load = [pltpu.make_async_copy(slope.at[at], slopes.at[at], sem.at[4, i])]
        store = [pltpu.make_async_copy(parts.at[at], dpre.at[at], sem.at[9, i])]
        for j, start in enumerate(starts):
            block = (pl.ds(start, rows), cols)
            load.append(
                pltpu.make_async_copy(ins[j].at[at], second.at[block], sem.at[j, i])
            )
            piece = (pl.ds(j * rows, rows), cols)
            store.append(
                pltpu.make_async_copy(terms.at[piece], outs[j].at[at], sem.at[5 + j, i])
            )
        for copy in load:
            copy.start()
        loads.append(load)
        stores.append(store)
    for (a, b), load, store in zip(cuts, loads, stores):
        for copy in load:
            copy.wait()
        part = (dot(grads[...], second[:, a:b]) * slopes[:, a:b]).astype(bf16)
        parts[:, a:b] = part
        for j, start in enumerate(starts):
            terms[j * rows : (j + 1) * rows, a:b] = dot(
                scaled_t[pl.ds(start, rows)], part
            ).astype(bf16)
        for copy in store:
            copy.start()
    for store in stores:
        for copy in store:
            copy.wait()


def back_kernel(dpre, first, scaled, ratio, own, other, gains):
    t, d = scaled.shape
    third = d // 3
    for j in range(3):
        cols = slice(j * third, (j + 1) * third)
        back = dot(dpre[...], first[cols], 1, 1)
        own[:, cols] = back[: t // 2]
        other[:, cols] = back[t // 2 :].astype(bf16)
        sums = jnp.sum(back * scaled[:, cols].astype(f32), axis=0, keepdims=True)
        gains[:, cols] = sums * ratio[:, cols]


WHOLE = pl.BlockSpec(memory_space=pltpu.VMEM)
AWAY = pl.BlockSpec(memory_space=pl.ANY)


def up(scaled, grads_t, first):
    t, d = scaled.shape
    half = first.shape[1]
    return pl.pallas_call(
        up_kernel,
        out_shape=(
            jax.ShapeDtypeStruct((t, half), f32),
            jax.ShapeDtypeStruct((d, half), bf16),
        ),
        in_specs=(WHOLE, WHOLE, AWAY),
        out_specs=(AWAY, AWAY),
        scratch_shapes=[
            pltpu.VMEM((d, half), bf16),
            pltpu.VMEM((t, half), f32),
            pltpu.VMEM((d, half), bf16),
            pltpu.SemaphoreType.DMA((3, len(tiles(half)))),
        ],
        compiler_params=VMEM,
        cost_estimate=pl.CostEstimate(
            flops=4 * t * d * half, bytes_accessed=4 * d * half, transcendentals=t * half
        ),
    )(scaled, grads_t, first)


def down(place, grads, scaled_t, slots, slope):
    t, wide = grads.shape
    rows, half = slots[0].shape
    return pl.pallas_call(
        down_kernel,
        out_shape=(jax.ShapeDtypeStruct((t, half), bf16),)
        + (jax.ShapeDtypeStruct((rows, half), bf16),) * 4,
        in_specs=[pl.BlockSpec(memory_space=pltpu.SMEM), WHOLE, WHOLE] + [AWAY] * 5,
        out_specs=(AWAY,) * 5,
        scratch_shapes=[
            pltpu.VMEM((wide, half), bf16),
            pltpu.VMEM((t, half), f32),
            pltpu.VMEM((t, half), bf16),
            pltpu.VMEM((wide, half), bf16),
            pltpu.SemaphoreType.DMA((10, len(tiles(half)))),
        ],
        compiler_params=VMEM,
        cost_estimate=pl.CostEstimate(
            flops=COST * t * wide * half, bytes_accessed=4 * wide * half, transcendentals=0
        ),
    )(place, grads, scaled_t, *slots, slope)


def back(dpre, first, scaled, ratio):
    t, d = scaled.shape
    half = first.shape[1]
    return pl.pallas_call(
        back_kernel,
        out_shape=(
            jax.ShapeDtypeStruct((t // 2, d), f32),
            jax.ShapeDtypeStruct((t // 2, d), bf16),
            jax.ShapeDtypeStruct((1, d), f32),
        ),
        compiler_params=VMEM,
        cost_estimate=pl.CostEstimate(
            flops=COST * t * d * half, bytes_accessed=4 * d * half, transcendentals=0
        ),
    )(dpre, first, scaled, ratio)


def selector(d, nz, nx):
    rows = d // (nz * nx)
    at = jnp.arange(nx * nz * PAD)
    block, line = at // PAD, at % PAD
    home = (block % nz * nx + block // nz) * rows + line
    home = jnp.where(line < rows, home, -1)
    return (jnp.arange(d)[:, None] == home[None]).astype(bf16)


def local(nz, nx, acts, grad_in, gain, w_in, w_out):
    x, y = lax.axis_index("x"), lax.axis_index("y")
    rows, hid = w_in.shape[1:]
    half = hid // 2
    tokens, d = acts.shape[1:]
    scale = 1.0 / jnp.sqrt(jnp.float32(tokens * nz * nx * 2))

    shards = []
    for w in (w_in[0], w_out[0]):
        mine, theirs = pick(y, w[:, :half], w[:, half:])
        top, bottom = pick(y, mine, shift(theirs, "y", 1))
        shards.append(jnp.concatenate([top, bottom], axis=0))
    block = jnp.pad(shards[1], ((0, PAD - 2 * rows), (0, 0)))
    step = shift(block, "z", 1), shift(block, "z", -1)
    first = direct_gather(shards[0], "x").reshape(nx * 2 * rows, half)
    first = lax.all_gather(after(first, *step), "z", axis=0, tiled=True)

    source = acts[0].astype(f32)
    centred = source - jnp.mean(source, axis=1, keepdims=True)
    inv = 1.0 / jnp.sqrt(jnp.mean(centred * centred, axis=1, keepdims=True) + 1e-06)
    normed = centred * inv
    scaled = (normed * gain[0][None, :]).astype(bf16)
    scaled = jnp.concatenate([scaled, shift(scaled, "y", 1)], axis=0)
    grads = jnp.concatenate([grad_in[0], shift(grad_in[0], "y", 1)], axis=0)
    chosen = selector(d, nz, nx)
    scaled_t = dot(chosen, scaled, 0, 1).astype(bf16)
    grads_w = dot(grads, chosen).astype(bf16)

    second = ring_gather(block, step, "z", [(), (), ()])
    slots = [second] + [shift(second, "x", -o) for o in SLOTS[1:]]
    scaled, first, grads_t = lax.optimization_barrier(
        (scaled, first, grads.T, second, scaled_t, grads_w)
    )[:3]
    slope, out_term = up(scaled, grads_t, first)
    sum_out = lax.psum_scatter(out_term, "z", scatter_dimension=0, tiled=True)
    place = jnp.stack([(x + o) % nx for o in SLOTS]).astype(jnp.int32)[None]
    dpre, *terms = down(place, grads_w, scaled_t, slots, slope)
    own, other, grad_g = back(dpre, first, scaled, scale / gain)
    grad_g = sum([shift(grad_g, "x", o) for o in SLOTS[1:]], grad_g)
    spare = grad_g.astype(bf16).reshape(3, d // 3)
    spare = jnp.pad(spare, ((2 * rows, PAD - 2 * rows - 3), (0, half - d // 3)))
    spare = jnp.broadcast_to(spare[None], (nz, PAD, half)).reshape(nz * PAD, half)
    spare = lax.optimization_barrier(spare)
    total_in = terms[0].astype(f32) + spare.astype(f32)
    for o, term in zip(SLOTS[1:], terms[1:]):
        total_in += shift(term, "x", o).astype(f32)
    sum_out, total_in = lax.optimization_barrier((sum_out, total_in.astype(bf16)))

    sum_out = sum_out.reshape(nx, 2 * rows, half)
    total_out = lax.dynamic_index_in_dim(sum_out, x, 0, keepdims=False).astype(f32)
    for o in SLOTS[1:]:
        part = lax.dynamic_index_in_dim(sum_out, (x + o) % nx, 0, keepdims=False)
        total_out += shift(part, "x", o).astype(f32)

    dscaled = own + after(shift(other, "y", 1), total_in).astype(f32)
    dnormed = dscaled * gain[0][None, :]
    grad_x = grad_in[0].astype(f32) + inv * (
        dnormed
        - jnp.mean(dnormed, axis=1, keepdims=True)
        - normed * jnp.mean(dnormed * normed, axis=1, keepdims=True)
    )
    route = [(2 * h + c, (2 * h + c - 1) % 4) for h in range(2) for c in range(2)]
    handed = lax.ppermute(grad_x.astype(bf16), ("h", "c"), route)

    total_in = lax.all_to_all(total_in.reshape(nz, PAD, half), "z", 0, 0)
    total_in = jnp.sum(total_in.astype(f32), axis=0)
    gain_rows = total_in[2 * rows : 2 * rows + 3]

    keeps, sends = zip(
        *(pick(y, w[:rows], w[rows : 2 * rows]) for w in (total_in * scale, total_out * scale))
    )
    got = shift(jnp.concatenate(sends + (gain_rows,), axis=0), "y", 1)
    grad_inw, grad_out = (
        jnp.concatenate(pick(y, keep, got[rows * i : rows * (i + 1)]), axis=1)
        for i, keep in enumerate(keeps)
    )
    grad_g = (gain_rows + got[2 * rows :])[:, : d // 3].reshape(1, d)
    return handed[None], grad_inw[None], grad_out[None], grad_g


def solution(mesh):
    nz, nx = 8, mesh.shape["dp"] // 16
    fine = Mesh(mesh.devices.reshape(nz, nx, 2, 2, 2), ("z", "x", "y", "h", "c"))
    wide = P(("h", "c"), ("z", "x", "y"), None)
    slim = P(("h", "c"), None)

    def run(*args):
        return local(nz, nx, *args)

    return jax.shard_map(
        run,
        mesh=fine,
        in_specs=(wide, wide, slim, wide, wide),
        out_specs=(wide, wide, wide, slim),
        check_vma=False,
    )
```

```python
import jax
import jax.numpy as jnp
from jax import lax
from jax.experimental import pallas as pl
from jax.experimental.pallas import tpu as pltpu
from jax.sharding import Mesh, PartitionSpec as P

coef = 0.7978845608
f32, bf16 = jnp.float32, jnp.bfloat16

SLOTS = (0, 1, 3, 2)
PAD = 40
COST = 200
VMEM = pltpu.CompilerParams(vmem_limit_bytes=56 * 1024 * 1024)


def shift(block, axis, distance):
    size = lax.axis_size(axis)
    return lax.ppermute(block, axis, [(i, (i + distance) % size) for i in range(size)])


def pick(flag, a, b):
    return jnp.where(flag == 0, a, b), jnp.where(flag == 0, b, a)


def ring_gather(block, first, axis, beside):
    size, r = lax.axis_size(axis), block.shape[0]
    me = lax.axis_index(axis)
    out = jnp.zeros((size * r, block.shape[1]), block.dtype)
    out = lax.dynamic_update_slice(out, block, (me * r, 0))
    right, left = first
    for k in range(1, size // 2 + 1):
        if k > 1:
            right, left = after(right, *beside[k - 2]), after(left, *beside[k - 2])
            right, left = shift(right, axis, 1), shift(left, axis, -1)
        out = lax.dynamic_update_slice(out, right, ((me - k) % size * r, 0))
        if k < size - k:
            out = lax.dynamic_update_slice(out, left, ((me + k) % size * r, 0))
    return out


def after(value, *others):
    return lax.optimization_barrier((value,) + others)[0]


def direct_gather(block, axis):
    size = lax.axis_size(axis)
    me = lax.axis_index(axis)
    out = jnp.zeros((size,) + block.shape, block.dtype)
    out = lax.dynamic_update_index_in_dim(out, block, me, 0)
    for k in range(1, size):
        got = shift(block, axis, k)
        out = lax.dynamic_update_index_in_dim(out, got, (me - k) % size, 0)
    return out


def dot(a, b, ca=1, cb=0):
    return lax.dot_general(a, b, (((ca,), (cb,)), ((), ())), preferred_element_type=f32)


def tiles(width):
    starts = list(range(0, width - 255, 256))
    ends = starts[1:] + [width]
    return list(zip(starts, ends))


def up_kernel(scaled, grads_t, first, slope, out_term, held, slopes, terms, sem):
    cuts = tiles(first.shape[1])
    loads, stores = [], []
    for i, (a, b) in enumerate(cuts):
        at = (slice(None), pl.ds(a, b - a))
        loads.append(pltpu.make_async_copy(first.at[at], held.at[at], sem.at[0, i]))
        stores.append(
            (
                pltpu.make_async_copy(slopes.at[at], slope.at[at], sem.at[1, i]),
                pltpu.make_async_copy(terms.at[at], out_term.at[at], sem.at[2, i]),
            )
        )
        loads[-1].start()
    for (a, b), load, (keep, send) in zip(cuts, loads, stores):
        load.wait()
        pre = dot(scaled[...], held[:, a:b])
        square = pre * pre
        part = 0.5 + 0.5 * jnp.tanh(pre * (coef + (coef * 0.044715) * square))
        slopes[:, a:b] = part + part * (1.0 - part) * (
            pre * (2.0 * coef + (2.0 * coef * 0.134145) * square)
        )
        keep.start()
        hidden = (pre * part).astype(bf16)
        terms[:, a:b] = dot(grads_t[...], hidden).astype(bf16)
        send.start()
    for pair in stores:
        for copy in pair:
            copy.wait()


def down_kernel(
    place, grads, scaled_t, s0, s1, s2, s3, slope, dpre, o0, o1, o2, o3,
    second, slopes, parts, terms, sem,
):
    rows = s0.shape[0]
    ins, outs = (s0, s1, s2, s3), (o0, o1, o2, o3)
    starts = [pl.multiple_of(place[0, j] * rows, rows) for j in range(4)]
    cuts = tiles(second.shape[1])
    loads, stores = [], []
    for i, (a, b) in enumerate(cuts):
        cols = pl.ds(a, b - a)
        at = (slice(None), cols)
        load = [pltpu.make_async_copy(slope.at[at], slopes.at[at], sem.at[4, i])]
        store = [pltpu.make_async_copy(parts.at[at], dpre.at[at], sem.at[9, i])]
        for j, start in enumerate(starts):
            block = (pl.ds(start, rows), cols)
            load.append(
                pltpu.make_async_copy(ins[j].at[at], second.at[block], sem.at[j, i])
            )
            piece = (pl.ds(j * rows, rows), cols)
            store.append(
                pltpu.make_async_copy(terms.at[piece], outs[j].at[at], sem.at[5 + j, i])
            )
        for copy in load:
            copy.start()
        loads.append(load)
        stores.append(store)
    for (a, b), load, store in zip(cuts, loads, stores):
        for copy in load:
            copy.wait()
        part = (dot(grads[...], second[:, a:b]) * slopes[:, a:b]).astype(bf16)
        parts[:, a:b] = part
        for j, start in enumerate(starts):
            terms[j * rows : (j + 1) * rows, a:b] = dot(
                scaled_t[pl.ds(start, rows)], part
            ).astype(bf16)
        for copy in store:
            copy.start()
    for store in stores:
        for copy in store:
            copy.wait()


def back_kernel(dpre, first, scaled, ratio, own, other, gains):
    t, d = scaled.shape
    third = d // 3
    for j in range(3):
        cols = slice(j * third, (j + 1) * third)
        back = dot(dpre[...], first[cols], 1, 1)
        own[:, cols] = back[: t // 2]
        other[:, cols] = back[t // 2 :].astype(bf16)
        sums = jnp.sum(back * scaled[:, cols].astype(f32), axis=0, keepdims=True)
        gains[:, cols] = sums * ratio[:, cols]


WHOLE = pl.BlockSpec(memory_space=pltpu.VMEM)
AWAY = pl.BlockSpec(memory_space=pl.ANY)


def up(scaled, grads_t, first):
    t, d = scaled.shape
    half = first.shape[1]
    return pl.pallas_call(
        up_kernel,
        out_shape=(
            jax.ShapeDtypeStruct((t, half), f32),
            jax.ShapeDtypeStruct((d, half), bf16),
        ),
        in_specs=(WHOLE, WHOLE, AWAY),
        out_specs=(AWAY, AWAY),
        scratch_shapes=[
            pltpu.VMEM((d, half), bf16),
            pltpu.VMEM((t, half), f32),
            pltpu.VMEM((d, half), bf16),
            pltpu.SemaphoreType.DMA((3, len(tiles(half)))),
        ],
        compiler_params=VMEM,
        cost_estimate=pl.CostEstimate(
            flops=4 * t * d * half, bytes_accessed=4 * d * half, transcendentals=t * half
        ),
    )(scaled, grads_t, first)


def down(place, grads, scaled_t, slots, slope):
    t, wide = grads.shape
    rows, half = slots[0].shape
    return pl.pallas_call(
        down_kernel,
        out_shape=(jax.ShapeDtypeStruct((t, half), bf16),)
        + (jax.ShapeDtypeStruct((rows, half), bf16),) * 4,
        in_specs=[pl.BlockSpec(memory_space=pltpu.SMEM), WHOLE, WHOLE] + [AWAY] * 5,
        out_specs=(AWAY,) * 5,
        scratch_shapes=[
            pltpu.VMEM((wide, half), bf16),
            pltpu.VMEM((t, half), f32),
            pltpu.VMEM((t, half), bf16),
            pltpu.VMEM((wide, half), bf16),
            pltpu.SemaphoreType.DMA((10, len(tiles(half)))),
        ],
        compiler_params=VMEM,
        cost_estimate=pl.CostEstimate(
            flops=COST * t * wide * half, bytes_accessed=4 * wide * half, transcendentals=0
        ),
    )(place, grads, scaled_t, *slots, slope)


def back(dpre, first, scaled, ratio):
    t, d = scaled.shape
    half = first.shape[1]
    return pl.pallas_call(
        back_kernel,
        out_shape=(
            jax.ShapeDtypeStruct((t // 2, d), f32),
            jax.ShapeDtypeStruct((t // 2, d), bf16),
            jax.ShapeDtypeStruct((1, d), f32),
        ),
        compiler_params=VMEM,
        cost_estimate=pl.CostEstimate(
            flops=COST * t * d * half, bytes_accessed=4 * d * half, transcendentals=0
        ),
    )(dpre, first, scaled, ratio)


def selector(d, nz, nx):
    rows = d // (nz * nx)
    at = jnp.arange(nx * nz * PAD)
    block, line = at // PAD, at % PAD
    home = (block % nz * nx + block // nz) * rows + line
    home = jnp.where(line < rows, home, -1)
    return (jnp.arange(d)[:, None] == home[None]).astype(bf16)


def local(nz, nx, acts, grad_in, gain, w_in, w_out):
    x, y = lax.axis_index("x"), lax.axis_index("y")
    rows, hid = w_in.shape[1:]
    half = hid // 2
    tokens, d = acts.shape[1:]
    scale = 1.0 / jnp.sqrt(jnp.float32(tokens * nz * nx * 2))

    shards = []
    for w in (w_in[0], w_out[0]):
        mine, theirs = pick(y, w[:, :half], w[:, half:])
        top, bottom = pick(y, mine, shift(theirs, "y", 1))
        shards.append(jnp.concatenate([top, bottom], axis=0))
    block = jnp.pad(shards[1], ((0, PAD - 2 * rows), (0, 0)))
    step = shift(block, "z", 1), shift(block, "z", -1)
    first = direct_gather(shards[0], "x").reshape(nx * 2 * rows, half)
    first = lax.all_gather(after(first, *step), "z", axis=0, tiled=True)

    source = acts[0].astype(f32)
    centred = source - jnp.mean(source, axis=1, keepdims=True)
    inv = 1.0 / jnp.sqrt(jnp.mean(centred * centred, axis=1, keepdims=True) + 1e-06)
    normed = centred * inv
    scaled = (normed * gain[0][None, :]).astype(bf16)
    scaled = jnp.concatenate([scaled, shift(scaled, "y", 1)], axis=0)
    grads = jnp.concatenate([grad_in[0], shift(grad_in[0], "y", 1)], axis=0)
    chosen = selector(d, nz, nx)
    scaled_t = dot(chosen, scaled, 0, 1).astype(bf16)
    grads_w = dot(grads, chosen).astype(bf16)

    second = ring_gather(block, step, "z", [(), (), ()])
    slots = [second] + [shift(second, "x", -o) for o in SLOTS[1:]]
    scaled, first, grads_t = lax.optimization_barrier(
        (scaled, first, grads.T, second, scaled_t, grads_w)
    )[:3]
    slope, out_term = up(scaled, grads_t, first)
    sum_out = lax.psum_scatter(out_term, "z", scatter_dimension=0, tiled=True)
    place = jnp.stack([(x + o) % nx for o in SLOTS]).astype(jnp.int32)[None]
    dpre, *terms = down(place, grads_w, scaled_t, slots, slope)
    own, other, grad_g = back(dpre, first, scaled, scale / gain)
    for distance in (1, 2, 4):
        grad_g += shift(grad_g, "z", distance)
    spare = jnp.pad(grad_g.reshape(3, d // 3), ((0, PAD - 2 * rows - 3), (0, half - d // 3)))
    spare = spare.astype(bf16)
    total_in = terms[0].astype(f32)
    for o, term in zip(SLOTS[1:], terms[1:]):
        total_in += shift(term, "x", o).astype(f32)
    sum_out, total_in = lax.optimization_barrier((sum_out, total_in.astype(bf16)))

    spare = jnp.broadcast_to(spare[None], (nx,) + spare.shape)
    sum_out = jnp.concatenate([sum_out.reshape(nx, 2 * rows, half), spare], axis=1)
    total_out = lax.dynamic_index_in_dim(sum_out, x, 0, keepdims=False).astype(f32)
    for o in SLOTS[1:]:
        part = lax.dynamic_index_in_dim(sum_out, (x + o) % nx, 0, keepdims=False)
        total_out += shift(part, "x", o).astype(f32)

    dscaled = own + after(shift(other, "y", 1), total_in).astype(f32)
    dnormed = dscaled * gain[0][None, :]
    grad_x = grad_in[0].astype(f32) + inv * (
        dnormed
        - jnp.mean(dnormed, axis=1, keepdims=True)
        - normed * jnp.mean(dnormed * normed, axis=1, keepdims=True)
    )
    route = [(2 * h + c, (2 * h + c - 1) % 4) for h in range(2) for c in range(2)]
    handed = lax.ppermute(grad_x.astype(bf16), ("h", "c"), route)

    total_in = lax.all_to_all(total_in.reshape(nz, PAD, half), "z", 0, 0)
    total_in = jnp.sum(total_in.astype(f32), axis=0)
    gain_rows = total_out[2 * rows : 2 * rows + 3]

    keeps, sends = zip(
        *(pick(y, w[:rows], w[rows : 2 * rows]) for w in (total_in * scale, total_out * scale))
    )
    got = shift(jnp.concatenate(sends + (gain_rows,), axis=0), "y", 1)
    grad_inw, grad_out = (
        jnp.concatenate(pick(y, keep, got[rows * i : rows * (i + 1)]), axis=1)
        for i, keep in enumerate(keeps)
    )
    grad_g = (gain_rows + got[2 * rows :])[:, : d // 3].reshape(1, d)
    return handed[None], grad_inw[None], grad_out[None], grad_g


def solution(mesh):
    nz, nx = 8, mesh.shape["dp"] // 16
    fine = Mesh(mesh.devices.reshape(nz, nx, 2, 2, 2), ("z", "x", "y", "h", "c"))
    wide = P(("h", "c"), ("z", "x", "y"), None)
    slim = P(("h", "c"), None)

    def run(*args):
        return local(nz, nx, *args)

    return jax.shard_map(
        run,
        mesh=fine,
        in_specs=(wide, wide, slim, wide, wide),
        out_specs=(wide, wide, wide, slim),
        check_vma=False,
    )
```

```python
import jax
import jax.numpy as jnp
from jax import lax
from jax.experimental import pallas as pl
from jax.experimental.pallas import tpu as pltpu
from jax.sharding import Mesh, PartitionSpec as P

coef = 0.7978845608
f32, bf16 = jnp.float32, jnp.bfloat16

SLOTS = (0, 1, 3, 2)
PAD = 40
COST = 200
VMEM = pltpu.CompilerParams(vmem_limit_bytes=56 * 1024 * 1024)


def shift(block, axis, distance):
    size = lax.axis_size(axis)
    return lax.ppermute(block, axis, [(i, (i + distance) % size) for i in range(size)])


def pick(flag, a, b):
    return jnp.where(flag == 0, a, b), jnp.where(flag == 0, b, a)


def ring_gather(block, first, axis, beside):
    size, r = lax.axis_size(axis), block.shape[0]
    me = lax.axis_index(axis)
    out = jnp.zeros((size * r, block.shape[1]), block.dtype)
    out = lax.dynamic_update_slice(out, block, (me * r, 0))
    right, left = first
    for k in range(1, size // 2 + 1):
        if k > 1:
            right, left = after(right, *beside[k - 2]), after(left, *beside[k - 2])
            right, left = shift(right, axis, 1), shift(left, axis, -1)
        out = lax.dynamic_update_slice(out, right, ((me - k) % size * r, 0))
        if k < size - k:
            out = lax.dynamic_update_slice(out, left, ((me + k) % size * r, 0))
    return out


def after(value, *others):
    return lax.optimization_barrier((value,) + others)[0]


def direct_gather(block, axis):
    size = lax.axis_size(axis)
    me = lax.axis_index(axis)
    out = jnp.zeros((size,) + block.shape, block.dtype)
    out = lax.dynamic_update_index_in_dim(out, block, me, 0)
    for k in range(1, size):
        got = shift(block, axis, k)
        out = lax.dynamic_update_index_in_dim(out, got, (me - k) % size, 0)
    return out


def dot(a, b, ca=1, cb=0):
    return lax.dot_general(a, b, (((ca,), (cb,)), ((), ())), preferred_element_type=f32)


TILE = 256


def cuts(width):
    return -(-width // TILE), width % TILE or TILE


def tile_loop(width, body):
    count, last = cuts(width)
    lax.fori_loop(
        0, count - 1, lambda i, _: body(i, pl.ds(pl.multiple_of(i * TILE, TILE), TILE)), None
    )
    body(count - 1, pl.ds((count - 1) * TILE, last))


def start_tiles(width, begin):
    count, last = cuts(width)
    for i in range(count):
        begin(i, pl.ds(i * TILE, TILE if i < count - 1 else last))


def up_kernel(scaled, grads_t, first, slope, out_term, held, slopes, terms, sem):
    width = first.shape[1]

    def load(i, cols):
        return pltpu.make_async_copy(first.at[:, cols], held.at[:, cols], sem.at[0, i])

    def keep(i, cols):
        return pltpu.make_async_copy(slopes.at[:, cols], slope.at[:, cols], sem.at[1, i])

    def send(i, cols):
        return pltpu.make_async_copy(terms.at[:, cols], out_term.at[:, cols], sem.at[2, i])

    def body(i, cols):
        load(i, cols).wait()
        pre = dot(scaled[...], held[:, cols])
        square = pre * pre
        part = 0.5 + 0.5 * jnp.tanh(pre * (coef + (coef * 0.044715) * square))
        slopes[:, cols] = part + part * (1.0 - part) * (
            pre * (2.0 * coef + (2.0 * coef * 0.134145) * square)
        )
        keep(i, cols).start()
        hidden = (pre * part).astype(bf16)
        terms[:, cols] = dot(grads_t[...], hidden).astype(bf16)
        send(i, cols).start()

    def finish(i, cols):
        keep(i, cols).wait()
        send(i, cols).wait()

    start_tiles(width, lambda i, cols: load(i, cols).start())
    tile_loop(width, body)
    start_tiles(width, finish)


def down_kernel(
    place, grads, scaled_t, s0, s1, s2, s3, slope, dpre, o0, o1, o2, o3,
    second, slopes, parts, terms, sem,
):
    rows, width = s0.shape
    ins, outs = (s0, s1, s2, s3), (o0, o1, o2, o3)

    def start(j):
        return pl.multiple_of(place[0, j] * rows, rows)

    def loads(i, cols):
        return [pltpu.make_async_copy(slope.at[:, cols], slopes.at[:, cols], sem.at[4, i])] + [
            pltpu.make_async_copy(
                ins[j].at[:, cols], second.at[pl.ds(start(j), rows), cols], sem.at[j, i]
            )
            for j in range(4)
        ]

    def stores(i, cols):
        return [pltpu.make_async_copy(parts.at[:, cols], dpre.at[:, cols], sem.at[9, i])] + [
            pltpu.make_async_copy(
                terms.at[pl.ds(j * rows, rows), cols], outs[j].at[:, cols], sem.at[5 + j, i]
            )
            for j in range(4)
        ]

    def body(i, cols):
        for copy in loads(i, cols):
            copy.wait()
        parts[:, cols] = (dot(grads[...], second[:, cols]) * slopes[:, cols]).astype(bf16)

        def term(j, _):
            to = pl.ds(pl.multiple_of(j * rows, rows), rows)
            terms[to, cols] = dot(scaled_t[pl.ds(start(j), rows)], parts[:, cols]).astype(bf16)

        lax.fori_loop(0, 4, term, None)
        for copy in stores(i, cols):
            copy.start()

    def begin(i, cols):
        for copy in loads(i, cols):
            copy.start()

    def finish(i, cols):
        for copy in stores(i, cols):
            copy.wait()

    start_tiles(width, begin)
    tile_loop(width, body)
    start_tiles(width, finish)


def back_kernel(dpre, first, scaled, ratio, own, other, gains):
    t, d = scaled.shape
    third = d // 3

    def body(j, _):
        cols = pl.ds(pl.multiple_of(j * third, third), third)
        back = dot(dpre[...], first[cols], 1, 1)
        own[:, cols] = back[: t // 2]
        other[:, cols] = back[t // 2 :].astype(bf16)
        sums = jnp.sum(back * scaled[:, cols].astype(f32), axis=0, keepdims=True)
        gains[:, cols] = sums * ratio[:, cols]

    lax.fori_loop(0, 3, body, None)


WHOLE = pl.BlockSpec(memory_space=pltpu.VMEM)
AWAY = pl.BlockSpec(memory_space=pl.ANY)


def up(scaled, grads_t, first):
    t, d = scaled.shape
    half = first.shape[1]
    return pl.pallas_call(
        up_kernel,
        out_shape=(
            jax.ShapeDtypeStruct((t, half), f32),
            jax.ShapeDtypeStruct((d, half), bf16),
        ),
        in_specs=(WHOLE, WHOLE, AWAY),
        out_specs=(AWAY, AWAY),
        scratch_shapes=[
            pltpu.VMEM((d, half), bf16),
            pltpu.VMEM((t, half), f32),
            pltpu.VMEM((d, half), bf16),
            pltpu.SemaphoreType.DMA((3, cuts(half)[0])),
        ],
        compiler_params=VMEM,
        cost_estimate=pl.CostEstimate(
            flops=4 * t * d * half, bytes_accessed=4 * d * half, transcendentals=t * half
        ),
    )(scaled, grads_t, first)


def down(place, grads, scaled_t, slots, slope):
    t, wide = grads.shape
    rows, half = slots[0].shape
    return pl.pallas_call(
        down_kernel,
        out_shape=(jax.ShapeDtypeStruct((t, half), bf16),)
        + (jax.ShapeDtypeStruct((rows, half), bf16),) * 4,
        in_specs=[pl.BlockSpec(memory_space=pltpu.SMEM), WHOLE, WHOLE] + [AWAY] * 5,
        out_specs=(AWAY,) * 5,
        scratch_shapes=[
            pltpu.VMEM((wide, half), bf16),
            pltpu.VMEM((t, half), f32),
            pltpu.VMEM((t, half), bf16),
            pltpu.VMEM((wide, half), bf16),
            pltpu.SemaphoreType.DMA((10, cuts(half)[0])),
        ],
        compiler_params=VMEM,
        cost_estimate=pl.CostEstimate(
            flops=COST * t * wide * half, bytes_accessed=4 * wide * half, transcendentals=0
        ),
    )(place, grads, scaled_t, *slots, slope)


def back(dpre, first, scaled, ratio):
    t, d = scaled.shape
    half = first.shape[1]
    return pl.pallas_call(
        back_kernel,
        out_shape=(
            jax.ShapeDtypeStruct((t // 2, d), f32),
            jax.ShapeDtypeStruct((t // 2, d), bf16),
            jax.ShapeDtypeStruct((1, d), f32),
        ),
        compiler_params=VMEM,
        cost_estimate=pl.CostEstimate(
            flops=COST * t * d * half, bytes_accessed=4 * d * half, transcendentals=0
        ),
    )(dpre, first, scaled, ratio)


def selector(d, nz, nx):
    rows = d // (nz * nx)
    at = jnp.arange(nx * nz * PAD)
    block, line = at // PAD, at % PAD
    home = (block % nz * nx + block // nz) * rows + line
    home = jnp.where(line < rows, home, -1)
    return (jnp.arange(d)[:, None] == home[None]).astype(bf16)


def local(nz, nx, acts, grad_in, gain, w_in, w_out):
    x, y = lax.axis_index("x"), lax.axis_index("y")
    rows, hid = w_in.shape[1:]
    half = hid // 2
    tokens, d = acts.shape[1:]
    scale = 1.0 / jnp.sqrt(jnp.float32(tokens * nz * nx * 2))

    shards = []
    for w in (w_in[0], w_out[0]):
        mine, theirs = pick(y, w[:, :half], w[:, half:])
        top, bottom = pick(y, mine, shift(theirs, "y", 1))
        shards.append(jnp.concatenate([top, bottom], axis=0))
    block = jnp.pad(shards[1], ((0, PAD - 2 * rows), (0, 0)))
    step = shift(block, "z", 1), shift(block, "z", -1)
    first = direct_gather(shards[0], "x").reshape(nx * 2 * rows, half)
    first = lax.all_gather(after(first, *step), "z", axis=0, tiled=True)

    source = acts[0].astype(f32)
    centred = source - jnp.mean(source, axis=1, keepdims=True)
    inv = 1.0 / jnp.sqrt(jnp.mean(centred * centred, axis=1, keepdims=True) + 1e-06)
    normed = centred * inv
    scaled = (normed * gain[0][None, :]).astype(bf16)
    scaled = jnp.concatenate([scaled, shift(scaled, "y", 1)], axis=0)
    grads = jnp.concatenate([grad_in[0], shift(grad_in[0], "y", 1)], axis=0)
    chosen = selector(d, nz, nx)
    scaled_t = dot(chosen, scaled, 0, 1).astype(bf16)
    grads_w = dot(grads, chosen).astype(bf16)

    second = ring_gather(block, step, "z", [(), (), ()])
    slots = [second] + [shift(second, "x", -o) for o in SLOTS[1:]]
    slope, out_term = up(after(scaled, second, scaled_t, grads_w), grads.T, first)
    sum_out = lax.psum_scatter(out_term, "z", scatter_dimension=0, tiled=True)
    place = jnp.stack([(x + o) % nx for o in SLOTS]).astype(jnp.int32)[None]
    dpre, *terms = down(place, grads_w, scaled_t, slots, slope)
    own, other, grad_g = back(dpre, first, scaled, scale / gain)
    for distance in (1, 2, 4):
        grad_g += shift(grad_g, "z", distance)
    spare = jnp.pad(grad_g.reshape(3, d // 3), ((0, PAD - 2 * rows - 3), (0, half - d // 3)))
    spare = spare.astype(bf16)
    total_in = terms[0].astype(f32)
    for o, term in zip(SLOTS[1:], terms[1:]):
        total_in += shift(term, "x", o).astype(f32)
    sum_out, total_in = lax.optimization_barrier((sum_out, total_in.astype(bf16)))

    spare = jnp.broadcast_to(spare[None], (nx,) + spare.shape)
    sum_out = jnp.concatenate([sum_out.reshape(nx, 2 * rows, half), spare], axis=1)
    total_out = lax.dynamic_index_in_dim(sum_out, x, 0, keepdims=False).astype(f32)
    for o in SLOTS[1:]:
        part = lax.dynamic_index_in_dim(sum_out, (x + o) % nx, 0, keepdims=False)
        total_out += shift(part, "x", o).astype(f32)

    dscaled = own + after(shift(other, "y", 1), total_in).astype(f32)
    dnormed = dscaled * gain[0][None, :]
    grad_x = grad_in[0].astype(f32) + inv * (
        dnormed
        - jnp.mean(dnormed, axis=1, keepdims=True)
        - normed * jnp.mean(dnormed * normed, axis=1, keepdims=True)
    )
    route = [(2 * h + c, (2 * h + c - 1) % 4) for h in range(2) for c in range(2)]
    handed = lax.ppermute(grad_x.astype(bf16), ("h", "c"), route)

    total_in = lax.all_to_all(total_in.reshape(nz, PAD, half), "z", 0, 0)
    total_in = jnp.sum(total_in.astype(f32), axis=0)
    gain_rows = total_out[2 * rows : 2 * rows + 3]

    keeps, sends = zip(
        *(pick(y, w[:rows], w[rows : 2 * rows]) for w in (total_in * scale, total_out * scale))
    )
    got = shift(jnp.concatenate(sends + (gain_rows,), axis=0), "y", 1)
    grad_inw, grad_out = (
        jnp.concatenate(pick(y, keep, got[rows * i : rows * (i + 1)]), axis=1)
        for i, keep in enumerate(keeps)
    )
    grad_g = (gain_rows + got[2 * rows :])[:, : d // 3].reshape(1, d)
    return handed[None], grad_inw[None], grad_out[None], grad_g


def solution(mesh):
    nz, nx = 8, mesh.shape["dp"] // 16
    fine = Mesh(mesh.devices.reshape(nz, nx, 2, 2, 2), ("z", "x", "y", "h", "c"))
    wide = P(("h", "c"), ("z", "x", "y"), None)
    slim = P(("h", "c"), None)

    def run(*args):
        return local(nz, nx, *args)

    return jax.shard_map(
        run,
        mesh=fine,
        in_specs=(wide, wide, slim, wide, wide),
        out_specs=(wide, wide, wide, slim),
        check_vma=False,
    )
```

```python
import jax
import jax.numpy as jnp
from jax import lax
from jax.experimental import pallas as pl
from jax.experimental.pallas import tpu as pltpu
from jax.sharding import Mesh, PartitionSpec as P

coef = 0.7978845608
f32, bf16 = jnp.float32, jnp.bfloat16

SLOTS = (0, 1, 3, 2)
PAD = 40
COST = 200
VMEM = pltpu.CompilerParams(vmem_limit_bytes=56 * 1024 * 1024)


def shift(block, axis, distance):
    size = lax.axis_size(axis)
    return lax.ppermute(block, axis, [(i, (i + distance) % size) for i in range(size)])


def pick(flag, a, b):
    return jnp.where(flag == 0, a, b), jnp.where(flag == 0, b, a)


def ring_gather(block, first, axis, beside):
    size, r = lax.axis_size(axis), block.shape[0]
    me = lax.axis_index(axis)
    out = jnp.zeros((size * r, block.shape[1]), block.dtype)
    out = lax.dynamic_update_slice(out, block, (me * r, 0))
    right, left = first
    for k in range(1, size // 2 + 1):
        if k > 1:
            right, left = after(right, *beside[k - 2]), after(left, *beside[k - 2])
            right, left = shift(right, axis, 1), shift(left, axis, -1)
        out = lax.dynamic_update_slice(out, right, ((me - k) % size * r, 0))
        if k < size - k:
            out = lax.dynamic_update_slice(out, left, ((me + k) % size * r, 0))
    return out


def after(value, *others):
    return lax.optimization_barrier((value,) + others)[0]


def direct_gather(block, axis):
    size = lax.axis_size(axis)
    me = lax.axis_index(axis)
    out = jnp.zeros((size,) + block.shape, block.dtype)
    out = lax.dynamic_update_index_in_dim(out, block, me, 0)
    for k in range(1, size):
        got = shift(block, axis, k)
        out = lax.dynamic_update_index_in_dim(out, got, (me - k) % size, 0)
    return out


def dot(a, b, ca=1, cb=0):
    return lax.dot_general(a, b, (((ca,), (cb,)), ((), ())), preferred_element_type=f32)


TILE = 512


def cuts(width):
    return -(-width // TILE), width % TILE or TILE


def tile_loop(width, body):
    count, last = cuts(width)
    lax.fori_loop(
        0, count - 1, lambda i, _: body(i, pl.ds(pl.multiple_of(i * TILE, TILE), TILE)), None
    )
    body(count - 1, pl.ds((count - 1) * TILE, last))


def start_tiles(width, begin):
    count, last = cuts(width)
    for i in range(count):
        begin(i, pl.ds(i * TILE, TILE if i < count - 1 else last))


def up_kernel(scaled, grads_t, first, slope, out_term, held, slopes, terms, sem):
    width = first.shape[1]

    def load(i, cols):
        return pltpu.make_async_copy(first.at[:, cols], held.at[:, cols], sem.at[0, i])

    def keep(i, cols):
        return pltpu.make_async_copy(slopes.at[:, cols], slope.at[:, cols], sem.at[1, i])

    def send(i, cols):
        return pltpu.make_async_copy(terms.at[:, cols], out_term.at[:, cols], sem.at[2, i])

    def body(i, cols):
        load(i, cols).wait()
        pre = dot(scaled[...], held[:, cols])
        square = pre * pre
        part = 0.5 + 0.5 * jnp.tanh(pre * (coef + (coef * 0.044715) * square))
        slopes[:, cols] = part + part * (1.0 - part) * (
            pre * (2.0 * coef + (2.0 * coef * 0.134145) * square)
        )
        keep(i, cols).start()
        hidden = (pre * part).astype(bf16)
        terms[:, cols] = dot(grads_t[...], hidden).astype(bf16)
        send(i, cols).start()

    def finish(i, cols):
        keep(i, cols).wait()
        send(i, cols).wait()

    start_tiles(width, lambda i, cols: load(i, cols).start())
    tile_loop(width, body)
    start_tiles(width, finish)


def down_kernel(
    place, grads, scaled_t, s0, s1, s2, s3, slope, dpre, o0, o1, o2, o3,
    second, slopes, parts, terms, sem,
):
    rows, width = s0.shape
    ins, outs = (s0, s1, s2, s3), (o0, o1, o2, o3)

    def start(j):
        return pl.multiple_of(place[0, j] * rows, rows)

    def loads(i, cols):
        return [pltpu.make_async_copy(slope.at[:, cols], slopes.at[:, cols], sem.at[4, i])] + [
            pltpu.make_async_copy(
                ins[j].at[:, cols], second.at[pl.ds(start(j), rows), cols], sem.at[j, i]
            )
            for j in range(4)
        ]

    def stores(i, cols):
        return [pltpu.make_async_copy(parts.at[:, cols], dpre.at[:, cols], sem.at[9, i])] + [
            pltpu.make_async_copy(
                terms.at[pl.ds(j * rows, rows), cols], outs[j].at[:, cols], sem.at[5 + j, i]
            )
            for j in range(4)
        ]

    def body(i, cols):
        for copy in loads(i, cols):
            copy.wait()
        parts[:, cols] = (dot(grads[...], second[:, cols]) * slopes[:, cols]).astype(bf16)

        def term(j, _):
            to = pl.ds(pl.multiple_of(j * rows, rows), rows)
            terms[to, cols] = dot(scaled_t[pl.ds(start(j), rows)], parts[:, cols]).astype(bf16)

        lax.fori_loop(0, 4, term, None)
        for copy in stores(i, cols):
            copy.start()

    def begin(i, cols):
        for copy in loads(i, cols):
            copy.start()

    def finish(i, cols):
        for copy in stores(i, cols):
            copy.wait()

    start_tiles(width, begin)
    tile_loop(width, body)
    start_tiles(width, finish)


def back_kernel(dpre, first, scaled, ratio, own, other, gains):
    t, d = scaled.shape
    third = d // 3

    def body(j, _):
        cols = pl.ds(pl.multiple_of(j * third, third), third)
        back = dot(dpre[...], first[cols], 1, 1)
        own[:, cols] = back[: t // 2]
        other[:, cols] = back[t // 2 :].astype(bf16)
        sums = jnp.sum(back * scaled[:, cols].astype(f32), axis=0, keepdims=True)
        gains[:, cols] = sums * ratio[:, cols]

    lax.fori_loop(0, 3, body, None)


WHOLE = pl.BlockSpec(memory_space=pltpu.VMEM)
AWAY = pl.BlockSpec(memory_space=pl.ANY)


def up(scaled, grads_t, first):
    t, d = scaled.shape
    half = first.shape[1]
    return pl.pallas_call(
        up_kernel,
        out_shape=(
            jax.ShapeDtypeStruct((t, half), f32),
            jax.ShapeDtypeStruct((d, half), bf16),
        ),
        in_specs=(WHOLE, WHOLE, AWAY),
        out_specs=(AWAY, AWAY),
        scratch_shapes=[
            pltpu.VMEM((d, half), bf16),
            pltpu.VMEM((t, half), f32),
            pltpu.VMEM((d, half), bf16),
            pltpu.SemaphoreType.DMA((3, cuts(half)[0])),
        ],
        compiler_params=VMEM,
        cost_estimate=pl.CostEstimate(
            flops=4 * t * d * half, bytes_accessed=4 * d * half, transcendentals=t * half
        ),
    )(scaled, grads_t, first)


def down(place, grads, scaled_t, slots, slope):
    t, wide = grads.shape
    rows, half = slots[0].shape
    return pl.pallas_call(
        down_kernel,
        out_shape=(jax.ShapeDtypeStruct((t, half), bf16),)
        + (jax.ShapeDtypeStruct((rows, half), bf16),) * 4,
        in_specs=[pl.BlockSpec(memory_space=pltpu.SMEM), WHOLE, WHOLE] + [AWAY] * 5,
        out_specs=(AWAY,) * 5,
        scratch_shapes=[
            pltpu.VMEM((wide, half), bf16),
            pltpu.VMEM((t, half), f32),
            pltpu.VMEM((t, half), bf16),
            pltpu.VMEM((wide, half), bf16),
            pltpu.SemaphoreType.DMA((10, cuts(half)[0])),
        ],
        compiler_params=VMEM,
        cost_estimate=pl.CostEstimate(
            flops=COST * t * wide * half, bytes_accessed=4 * wide * half, transcendentals=0
        ),
    )(place, grads, scaled_t, *slots, slope)


def back(dpre, first, scaled, ratio):
    t, d = scaled.shape
    half = first.shape[1]
    return pl.pallas_call(
        back_kernel,
        out_shape=(
            jax.ShapeDtypeStruct((t // 2, d), f32),
            jax.ShapeDtypeStruct((t // 2, d), bf16),
            jax.ShapeDtypeStruct((1, d), f32),
        ),
        compiler_params=VMEM,
        cost_estimate=pl.CostEstimate(
            flops=COST * t * d * half, bytes_accessed=4 * d * half, transcendentals=0
        ),
    )(dpre, first, scaled, ratio)


def selector(d, nz, nx):
    rows = d // (nz * nx)
    at = jnp.arange(nx * nz * PAD)
    block, line = at // PAD, at % PAD
    home = (block % nz * nx + block // nz) * rows + line
    home = jnp.where(line < rows, home, -1)
    return (jnp.arange(d)[:, None] == home[None]).astype(bf16)


def local(nz, nx, acts, grad_in, gain, w_in, w_out):
    x, y = lax.axis_index("x"), lax.axis_index("y")
    rows, hid = w_in.shape[1:]
    half = hid // 2
    tokens, d = acts.shape[1:]
    scale = 1.0 / jnp.sqrt(jnp.float32(tokens * nz * nx * 2))

    shards = []
    for w in (w_in[0], w_out[0]):
        mine, theirs = pick(y, w[:, :half], w[:, half:])
        top, bottom = pick(y, mine, shift(theirs, "y", 1))
        shards.append(jnp.concatenate([top, bottom], axis=0))
    block = jnp.pad(shards[1], ((0, PAD - 2 * rows), (0, 0)))
    step = shift(block, "z", 1), shift(block, "z", -1)
    first = direct_gather(shards[0], "x").reshape(nx * 2 * rows, half)
    first = lax.all_gather(after(first, *step), "z", axis=0, tiled=True)

    source = acts[0].astype(f32)
    centred = source - jnp.mean(source, axis=1, keepdims=True)
    inv = 1.0 / jnp.sqrt(jnp.mean(centred * centred, axis=1, keepdims=True) + 1e-06)
    normed = centred * inv
    scaled = (normed * gain[0][None, :]).astype(bf16)
    scaled = jnp.concatenate([scaled, shift(scaled, "y", 1)], axis=0)
    grads = jnp.concatenate([grad_in[0], shift(grad_in[0], "y", 1)], axis=0)
    chosen = selector(d, nz, nx)
    scaled_t = dot(chosen, scaled, 0, 1).astype(bf16)
    grads_w = dot(grads, chosen).astype(bf16)

    second = ring_gather(block, step, "z", [(), (), ()])
    slots = [second] + [shift(second, "x", -o) for o in SLOTS[1:]]
    slope, out_term = up(after(scaled, second, scaled_t, grads_w), grads.T, first)
    sum_out = lax.psum_scatter(out_term, "z", scatter_dimension=0, tiled=True)
    place = jnp.stack([(x + o) % nx for o in SLOTS]).astype(jnp.int32)[None]
    dpre, *terms = down(place, grads_w, scaled_t, slots, slope)
    own, other, grad_g = back(dpre, first, scaled, scale / gain)
    for distance in (1, 2, 4):
        grad_g += shift(grad_g, "z", distance)
    spare = jnp.pad(grad_g.reshape(3, d // 3), ((0, PAD - 2 * rows - 3), (0, half - d // 3)))
    spare = spare.astype(bf16)
    total_in = terms[0].astype(f32)
    for o, term in zip(SLOTS[1:], terms[1:]):
        total_in += shift(term, "x", o).astype(f32)
    sum_out, total_in = lax.optimization_barrier((sum_out, total_in.astype(bf16)))

    spare = jnp.broadcast_to(spare[None], (nx,) + spare.shape)
    sum_out = jnp.concatenate([sum_out.reshape(nx, 2 * rows, half), spare], axis=1)
    total_out = lax.dynamic_index_in_dim(sum_out, x, 0, keepdims=False).astype(f32)
    for o in SLOTS[1:]:
        part = lax.dynamic_index_in_dim(sum_out, (x + o) % nx, 0, keepdims=False)
        total_out += shift(part, "x", o).astype(f32)

    dscaled = own + after(shift(other, "y", 1), total_in).astype(f32)
    dnormed = dscaled * gain[0][None, :]
    grad_x = grad_in[0].astype(f32) + inv * (
        dnormed
        - jnp.mean(dnormed, axis=1, keepdims=True)
        - normed * jnp.mean(dnormed * normed, axis=1, keepdims=True)
    )
    route = [(2 * h + c, (2 * h + c - 1) % 4) for h in range(2) for c in range(2)]
    handed = lax.ppermute(grad_x.astype(bf16), ("h", "c"), route)

    total_in = lax.all_to_all(total_in.reshape(nz, PAD, half), "z", 0, 0)
    total_in = jnp.sum(total_in.astype(f32), axis=0)
    gain_rows = total_out[2 * rows : 2 * rows + 3]

    keeps, sends = zip(
        *(pick(y, w[:rows], w[rows : 2 * rows]) for w in (total_in * scale, total_out * scale))
    )
    got = shift(jnp.concatenate(sends + (gain_rows,), axis=0), "y", 1)
    grad_inw, grad_out = (
        jnp.concatenate(pick(y, keep, got[rows * i : rows * (i + 1)]), axis=1)
        for i, keep in enumerate(keeps)
    )
    grad_g = (gain_rows + got[2 * rows :])[:, : d // 3].reshape(1, d)
    return handed[None], grad_inw[None], grad_out[None], grad_g


def solution(mesh):
    nz, nx = 8, mesh.shape["dp"] // 16
    fine = Mesh(mesh.devices.reshape(nz, nx, 2, 2, 2), ("z", "x", "y", "h", "c"))
    wide = P(("h", "c"), ("z", "x", "y"), None)
    slim = P(("h", "c"), None)

    def run(*args):
        return local(nz, nx, *args)

    return jax.shard_map(
        run,
        mesh=fine,
        in_specs=(wide, wide, slim, wide, wide),
        out_specs=(wide, wide, wide, slim),
        check_vma=False,
    )
```
